32 devices in a mesh: rows: 16 (over z, x, core), dates: 2 (over y).
Axes of the slice: x: 2, y: 2, z: 4, core: 2. Of those that a mesh axis runs over, the one named last changes fastest.
Arguments:
- obs_mask: int32 [16, 128, 4096], P('dates', 'rows'), may hold values 0 or 1
- precision: float32 [16, 128, 4096], P('dates', 'rows'), may hold values from 0.5 to 4
- observed: float32 [16, 128, 4096], P('dates', 'rows')
- edge_class: int32 [2, 128, 4096], P(None, 'rows'), may hold values from 0 to 7
- temporal_weight: float32 [15], replicated, may hold values from 0.5 to 4
- inverse: bfloat16 [16, 16, 128, 4096], P(None, None, 'rows', 'dates'), as said below
Outputs:
- solution: float32 [16, 128, 4096], P('dates', 'rows')
- residual: float32 [16, 128, 4096], P('dates', 'rows')
The draws below stay inside these ranges and needn't reach their ends.
Inputs may be any that keep to these rules, and one draw needn't show every extreme that they name: `inverse`: each pixel's matrix is symmetric with a diagonal larger than the sum of magnitudes of its row's other entries.
All inputs are finite; a program needn't handle non-finite values. No bound on the sum of `obs_mask` on one device may be relied on, other than what follows from the above.
Results may differ from the reference program's by a relative error of at most 0.0065.
Values sent between devices are 32-bit elements; how exact they have to be, the bound alone decides.
No kernel may reach another device: no remote copies, remote signals or barrier semaphores. Data moves between devices by JAX's collectives and lax.ppermute only.
A program may use at most 64 MiB of HBM per device.

```python
import math
import jax
import jax.numpy as jnp
from jax import lax

COLS = 4096
DATES = 16
ITERS = 2
LINES = 128


def draw_observed(key, part):
    first, second = jax.random.split(key)
    shape = (DATES, LINES, COLS)
    row_ids = lax.broadcasted_iota(jnp.int32, shape, 1).astype(jnp.float32)
    ramp = 1.0 + 2.0 * row_ids / max(LINES - 1, 1)
    rough = jnp.exp(jax.random.uniform(second, shape, jnp.float32, -0.7, 0.7))
    base = jnp.clip(jax.random.normal(first, shape, jnp.float32), -4.0, 4.0)
    return (base * ramp * rough).astype(jnp.float32)


def draw_inverse(key, part):
    first, second = jax.random.split(key)
    off = jax.random.uniform(first, (DATES, DATES, LINES, COLS), jnp.float32, -0.3, 0.3)
    sym = 0.5 * (off + jnp.swapaxes(off, 0, 1))
    diag = 5.0 + jax.random.uniform(second, (DATES, LINES, COLS), jnp.float32, 0.0, 2.0)
    eye = lax.broadcasted_iota(jnp.int32, (DATES, DATES, 1, 1), 0) == lax.broadcasted_iota(jnp.int32, (DATES, DATES, 1, 1), 1)
    full = jnp.where(eye, diag[:, None, :, :], sym)
    return full.astype(jnp.bfloat16)


def with_ends(values, stream_key, low, largest):
    shape = values.shape
    place = [jax.random.randint(jax.random.fold_in(stream_key, axis), (), 0, shape[axis]) for axis in range(len(shape))]
    values = values.at[tuple(place)].set(low)
    longest = shape.index(max(shape))
    place[longest] = (place[longest] + 1) % shape[longest]
    return values.at[tuple(place)].set(largest)


def shard_levels(stream_key, extent, cuts, low, top_value):
    def one(dim, blocks):
        steps = jax.random.uniform(jax.random.fold_in(jax.random.fold_in(stream_key, 6), dim), (blocks,), jnp.float32, low / len(cuts), top_value / len(cuts))
        return jnp.repeat(jnp.exp(steps), extent[dim] // blocks).reshape((-1,) + (1,) * (len(extent) - dim - 1))

    factor_of = one(*cuts[0])
    for cut in cuts[1:]:
        factor_of = factor_of * one(*cut)
    return factor_of


def setup_inputs(seed: int = 0) -> dict:
    streams_of = jax.random.split(jax.random.key(seed), 7)
    return {
        "obs_mask": with_ends((jax.random.randint(streams_of[0], (DATES, LINES, COLS), 0, 5) < 3).astype(jnp.int32), jax.random.fold_in(streams_of[0], 1), 0, 1),
        "precision": jnp.clip(jnp.exp(math.log(4.0) - 2.0794415 * jax.random.uniform(streams_of[1], (DATES, LINES, COLS), jnp.float32) ** shard_levels(streams_of[1], (DATES, LINES, COLS), ((0, 2), (1, 16)), -0.2, 0.2)), 0.5, 4.0),
        "observed": draw_observed(jax.random.fold_in(streams_of[6], 71), 0),
        "edge_class": with_ends(jax.random.randint(streams_of[3], (2, LINES, COLS), 0, 8), jax.random.fold_in(streams_of[3], 1), 0, 7).astype(jnp.int32),
        "temporal_weight": jnp.clip(jnp.exp(jax.random.uniform(streams_of[4], (DATES - 1,), jnp.float32, math.log(0.5), math.log(4.0))), 0.5, 4.0),
        "inverse": draw_inverse(jax.random.fold_in(streams_of[6], 71), 0),
    }


mass_term = 0.1


def edge_weights(edge_class, line_start, lines_total):
    classes = edge_class.astype(jnp.float32)
    rows_here = edge_class.shape[1]
    columns = edge_class.shape[2]
    col_ids = lax.broadcasted_iota(jnp.int32, (rows_here, columns), 1)
    row_ids = lax.broadcasted_iota(jnp.int32, (rows_here, columns), 0) + line_start
    across = jnp.where(col_ids == columns - 1, 0.0, 0.25 * (classes[0] + 1.0))
    downward = jnp.where(row_ids == lines_total - 1, 0.0, 0.25 * (classes[1] + 1.0))
    return across, downward


def operate(field, padded, data_weight, across, across_prev, downward, downward_prev, tau_up, tau_down):
    total = (mass_term + data_weight) * field
    total = total + across * (field - padded[1:-1, 1:-1, 2:]) + across_prev * (field - padded[1:-1, 1:-1, :-2])
    total = total + downward * (field - padded[1:-1, 2:, 1:-1]) + downward_prev * (field - padded[1:-1, :-2, 1:-1])
    total = total + tau_up * (field - padded[2:, 1:-1, 1:-1]) + tau_down * (field - padded[:-2, 1:-1, 1:-1])
    return total


def apply_inverse(inverse, values):
    total = inverse[:, 0].astype(jnp.float32) * values[0][None]
    for source in range(1, values.shape[0]):
        total = total + inverse[:, source].astype(jnp.float32) * values[source][None]
    return total


def reference(obs_mask, precision, observed, edge_class, temporal_weight, inverse):
    data_weight = obs_mask.astype(jnp.float32) * precision
    rhs = data_weight * observed
    across, downward = edge_weights(edge_class, 0, edge_class.shape[1])
    across_prev = jnp.pad(across, ((0, 0), (1, 0)))[:, :-1]
    downward_prev = jnp.pad(downward, ((1, 0), (0, 0)))[:-1]
    zero_one = jnp.zeros((1,), jnp.float32)
    tau_ext = jnp.concatenate([zero_one, temporal_weight, zero_one])
    tau_up = tau_ext[1:][:, None, None]
    tau_down = tau_ext[:-1][:, None, None]

    def operator(field):
        return operate(field, jnp.pad(field, 1), data_weight, across, across_prev, downward, downward_prev, tau_up, tau_down)

    solution = jnp.zeros_like(rhs)
    residual = rhs
    precond = apply_inverse(inverse, residual)
    search = precond
    rz_now = jnp.sum(residual * precond)
    for iteration in range(ITERS):
        image = operator(search)
        alpha = rz_now / jnp.sum(search * image)
        solution = solution + alpha * search
        residual = residual - alpha * image
        if iteration + 1 < ITERS:
            precond = apply_inverse(inverse, residual)
            rz_next = jnp.sum(residual * precond)
            search = precond + (rz_next / rz_now) * search
            rz_now = rz_next
    return solution, residual
```

```python
import functools

import jax
import jax.numpy as jnp
from jax import lax
from jax.experimental import pallas as pl
from jax.experimental.pallas import tpu as pltpu
from jax.sharding import PartitionSpec as P

MASS = 0.1
LANES = 128
VMEM = pl.BlockSpec(memory_space=pltpu.VMEM)
SMEM = pl.BlockSpec(memory_space=pltpu.SMEM)
PARAMS = pltpu.CompilerParams(vmem_limit_bytes=32 * 1024 * 1024)


def call(kernel, out_shapes, scratch, scalars, arrays):
    return pl.pallas_call(
        kernel,
        out_shape=[jax.ShapeDtypeStruct(shape, jnp.float32) for shape in out_shapes],
        in_specs=[SMEM] * len(scalars) + [VMEM] * len(arrays),
        out_specs=[VMEM] * len(out_shapes),
        scratch_shapes=[pltpu.VMEM(shape, jnp.float32) for shape in scratch],
        compiler_params=PARAMS,
    )(*scalars, *arrays)


def tile(index):
    return pl.ds(pl.multiple_of(index * LANES, LANES), LANES)


def columns(block, width):
    return pl.ds(pl.multiple_of(block * width, LANES), width)


def row_ids(width):
    return lax.broadcasted_iota(jnp.int32, (8, width), 0)


def lane_ids(width):
    return lax.broadcasted_iota(jnp.int32, (8, width), 1)


def window_start(block, dates_here, length, dates):
    return jnp.clip(block * dates_here - 1, 0, dates - length)


def edge_rows(value, parity):
    top, bottom = value[0:1], value[7:8]
    return jnp.where(parity == 0, bottom, top), jnp.where(parity == 0, top, bottom)


def halo_rows(first, second, parity):
    above = jnp.where(parity == 0, second, first)
    below = jnp.where(parity == 0, first, second)
    return above, below


def stencil(value, above, below, left, right, later, earlier, weights, diagonal, tau_up, tau_down):
    across, across_prev, downward, downward_prev = weights
    width = value.shape[1]
    rows, lanes = row_ids(width), lane_ids(width)
    next_column = jnp.where(lanes == width - 1, right, pltpu.roll(value, width - 1, 1))
    prev_column = jnp.where(lanes == 0, left, pltpu.roll(value, 1, 1))
    next_row = jnp.where(rows == 7, below, pltpu.roll(value, 7, 0))
    prev_row = jnp.where(rows == 0, above, pltpu.roll(value, 1, 0))
    away = across * next_column + across_prev * prev_column
    away = away + downward * next_row + downward_prev * prev_row
    return diagonal * value - (away + tau_up * later + tau_down * earlier)


def apply_inverse(inverse, source, store, first_total):
    dates = inverse.shape[0]

    def step(index, total):
        lanes = tile(index)
        values = [source[s, :, lanes] for s in range(dates)]
        for t in range(dates):
            mapped = inverse[t, 0, :, lanes].astype(jnp.float32) * values[0]
            for s in range(1, dates):
                mapped = mapped + inverse[t, s, :, lanes].astype(jnp.float32) * values[s]
            total = total + values[t] * mapped
            store(t, lanes, mapped)
        return total

    return lax.fori_loop(0, source.shape[2] // LANES, step, first_total)


def pack_edges(field, parity, first, second, ends):
    dates, _, width = field.shape
    lanes = lane_ids(LANES)
    begin = jnp.zeros((8, LANES), jnp.float32)
    end = begin
    for t in range(dates):
        value = field[t]
        send_1, send_2 = edge_rows(value, parity)
        first[t : t + 1, :] = send_1
        second[t : t + 1, :] = send_2
        begin = jnp.where(lanes == t, value[:, 0:1], begin)
        end = jnp.where(lanes == t, value[:, width - 1 : width], end)
    ends[0:8, :] = begin
    ends[8:16, :] = end


def gather_dates(target, own, received, date_block, blocks, dates_here):
    for j in range(dates_here):
        target[date_block * dates_here + j] = own(j)
    for k in range(1, blocks):
        source = lax.rem(date_block + blocks - k, blocks)
        for j in range(dates_here):
            target[source * dates_here + j] = received[k - 1, j]


def send_windows(field, windows, date_block, blocks, dates_here):
    length = windows.shape[1]
    for k in range(1, blocks):
        target = lax.rem(date_block + k, blocks)
        start = window_start(target, dates_here, length, field.shape[0])
        for j in range(length):
            windows[k - 1, j] = field[start + j]


def first_kernel(blocks, place, mask, precision, observed, received, inverse, precond, first, second, ends, windows, dot, rhs):
    date_block, parity = place[0], place[1]
    dates_here = observed.shape[0]
    here = columns(date_block, rhs.shape[2])

    def own(j):
        return mask[j, :, here].astype(jnp.float32) * precision[j, :, here] * observed[j, :, here]

    gather_dates(rhs, own, received, date_block, blocks, dates_here)

    def store(t, lanes, value):
        precond[t, :, lanes] = value

    dot[...] = apply_inverse(inverse, rhs, store, jnp.zeros((8, LANES), jnp.float32))
    pack_edges(precond, parity, first, second, ends)
    send_windows(precond, windows, date_block, blocks, dates_here)


def pixel_image(place, tau, weights_all, field, halo_1, halo_2, ends_left, ends_right, data_weight, use):
    date_block, parity = place[0], place[1]
    dates, _, width = field.shape
    here = columns(date_block, width)
    weights = [weights_all[k, :, here] for k in range(4)]
    weight_sum = weights_all[4, :, here]
    for t in range(dates):
        above, below = halo_rows(halo_1[t : t + 1, :], halo_2[t : t + 1, :], parity)
        tau_up, tau_down = tau[t + 1], tau[t]
        value = field[t]
        diagonal = weight_sum + data_weight[t] + (tau_up + tau_down)
        image = stencil(
            value,
            above,
            below,
            ends_left[:, t : t + 1],
            ends_right[:, t : t + 1],
            field[min(t + 1, dates - 1)],
            field[max(t - 1, 0)],
            weights,
            diagonal,
            tau_up,
            tau_down,
        )
        use(t, value, image)


def fold(value):
    total = value[:, :LANES]
    for index in range(1, value.shape[1] // LANES):
        total = total + value[:, index * LANES : (index + 1) * LANES]
    return total


def second_kernel(
    blocks, place, tau, weights, precond, halo_1, halo_2, ends_left, ends_right, mask, precision, received, inverse,
    mapped, first, second, ends, windows, edges, data_weight, dot_image, dot_mapped, image_all, total,
):
    date_block, parity = place[0], place[1]
    dates_here = mask.shape[0]
    here = columns(date_block, precond.shape[2])

    def own(j):
        return mask[j, :, here].astype(jnp.float32) * precision[j, :, here]

    gather_dates(data_weight, own, received, date_block, blocks, dates_here)
    total[...] = jnp.zeros_like(total)

    def use(t, value, image):
        image_all[t] = image
        total[...] = total[...] + fold(value * image)

    pixel_image(place, tau, weights, precond, halo_1, halo_2, ends_left, ends_right, data_weight, use)
    dot_image[...] = total[...]

    def store(t, lanes, value):
        mapped[t, :, lanes] = value

    dot_mapped[...] = apply_inverse(inverse, image_all, store, jnp.zeros((8, LANES), jnp.float32))
    pack_edges(mapped, parity, first, second, ends)
    send_windows(mapped, windows, date_block, blocks, dates_here)
    for k in range(1, blocks):
        target = lax.rem(date_block + k, blocks)
        for j in range(dates_here):
            send_1, send_2 = edge_rows(mapped[target * dates_here + j], parity)
            edges[k - 1, j : j + 1, :] = send_1
            edges[k - 1, dates_here + j : dates_here + j + 1, :] = send_2


def third_kernel(place, tau, weights, mapped, halo_1, halo_2, ends_left, ends_right, data_weight, dot_1, dot_2, dot_3, sums, total):
    total[...] = jnp.zeros_like(total)

    def use(t, value, image):
        total[...] = total[...] + fold(value * image)

    pixel_image(place, tau, weights, mapped, halo_1, halo_2, ends_left, ends_right, data_weight, use)
    rows = row_ids(LANES)
    result = jnp.zeros((8, LANES), jnp.float32)
    for index, dot in enumerate((dot_1, dot_2, dot_3, total)):
        result = jnp.where(rows == index, jnp.sum(dot[...]), result)
    sums[...] = result


def last_kernel(
    blocks, place, tau, weights_all, sums, precond, mapped, precond_other, mapped_other, own_p1, own_p2, own_m1, own_m2,
    other_1, other_2, mask, precision, observed, solution, residual, field, above_all, below_all,
):
    date_block, parity = place[0], place[1]
    dates, _, width = precond.shape
    dates_here, _, all_columns = observed.shape
    length = field.shape[0]
    one = sums[0:1, :]
    two = sums[1:2, :]
    three = sums[2:3, :]
    four = sums[3:4, :]
    alpha = one / two
    rz = alpha * alpha * three - one
    ahead = 1.0 + rz / one
    curve = ahead * ahead * two - 2.0 * ahead * alpha * three + alpha * alpha * four
    alpha_last = rz / curve
    scale_p = jnp.tile(alpha + alpha_last * ahead, (1, width // LANES))
    scale_m = jnp.tile(-alpha_last * alpha, (1, width // LANES))

    def mix(p, m):
        return scale_p * p + scale_m * m

    start = window_start(date_block, dates_here, length, dates)
    offset = date_block * dates_here - start
    here = columns(date_block, width)
    for j in range(length):
        field[j, :, here] = mix(precond[start + j], mapped[start + j])
    for j in range(dates_here):
        date = pl.ds(date_block * dates_here + j, 1)
        above, below = halo_rows(mix(own_p1[date, :], own_m1[date, :]), mix(own_p2[date, :], own_m2[date, :]), parity)
        above_all[j : j + 1, here] = above
        below_all[j : j + 1, here] = below
    for k in range(1, blocks):
        there = columns(lax.rem(date_block + blocks - k, blocks), width)
        for j in range(length):
            field[j, :, there] = mix(precond_other[k - 1, j], mapped_other[k - 1, j])
        for j in range(dates_here):
            p, m = slice(j, j + 1), slice(dates_here + j, dates_here + j + 1)
            above, below = halo_rows(
                mix(other_1[k - 1, p, :], other_1[k - 1, m, :]), mix(other_2[k - 1, p, :], other_2[k - 1, m, :]), parity
            )
            above_all[j : j + 1, there] = above
            below_all[j : j + 1, there] = below
    weights = [weights_all[k] for k in range(4)]
    weight_sum = weights_all[4]
    for j in range(dates_here):
        tau_up, tau_down = tau[date_block * dates_here + j + 1], tau[date_block * dates_here + j]
        data_weight = mask[j].astype(jnp.float32) * precision[j]
        place_j = offset + j
        value = field[place_j]
        image = stencil(
            value,
            above_all[j : j + 1, :],
            below_all[j : j + 1, :],
            0.0,
            0.0,
            field[jnp.minimum(place_j + 1, length - 1)],
            field[jnp.maximum(place_j - 1, 0)],
            weights,
            weight_sum + data_weight + (tau_up + tau_down),
            tau_up,
            tau_down,
        )
        solution[j] = value
        residual[j] = data_weight * observed[j] - image


def body(blocks, slabs, obs_mask, precision, observed, edge_class, temporal_weight, inverse):
    dates_here, lines, all_columns = observed.shape
    dates = inverse.shape[0]
    width = all_columns // blocks
    length = min(dates_here + (1 if blocks == 2 else 2), dates)
    line_block = lax.axis_index("rows")
    date_block = lax.axis_index("dates")
    parity = lax.rem(line_block, 2)
    place = jnp.stack([date_block, parity]).astype(jnp.int32)

    pairs = [(i, i ^ 1) for i in range(slabs)]
    across_pairs = [(i, i + 1) for i in range(1, slabs - 1, 2)]
    across_pairs = across_pairs + [(b, a) for a, b in across_pairs]

    def rotate(value, k):
        return lax.ppermute(value, "dates", [(i, (i + k) % blocks) for i in range(blocks)])

    def swap_rows(first, second):
        return lax.ppermute(first, "rows", pairs), lax.ppermute(second, "rows", across_pairs)

    def swap_ends(ends):
        if blocks == 2:
            other = rotate(ends, 1)
            return other[8:16], other[0:8]
        forward = [(i, i + 1) for i in range(blocks - 1)]
        backward = [(b, a) for a, b in forward]
        return lax.ppermute(ends[8:16], "dates", forward), lax.ppermute(ends[0:8], "dates", backward)

    def send(stack):
        return jnp.stack([rotate(stack[k - 1], k) for k in range(1, blocks)])

    def part(value, k):
        there = lax.rem(date_block + k, blocks) * width
        return lax.dynamic_slice_in_dim(value, there, width, 2)

    def weight(k):
        return part(obs_mask, k).astype(jnp.float32) * part(precision, k)

    rhs_other = jnp.stack([rotate(weight(k) * part(observed, k), k) for k in range(1, blocks)])
    weight_other = jnp.stack([rotate(weight(k), k) for k in range(1, blocks)])

    classes = edge_class.astype(jnp.float32)
    col_ids = lax.broadcasted_iota(jnp.int32, (lines, all_columns), 1)
    line_ids = lax.broadcasted_iota(jnp.int32, (lines, all_columns), 0) + line_block * lines
    across = jnp.where(col_ids == all_columns - 1, 0.0, 0.25 * (classes[0] + 1.0))
    downward = jnp.where(line_ids == lines * slabs - 1, 0.0, 0.25 * (classes[1] + 1.0))
    across_prev = jnp.pad(across, ((0, 0), (1, 0)))[:, :-1]
    above_row = lax.ppermute(downward[-1:], "rows", [(i, i + 1) for i in range(slabs - 1)])
    downward_prev = jnp.concatenate([above_row, downward[:-1]], axis=0)
    weights = jnp.stack([across, across_prev, downward, downward_prev, MASS + across + across_prev + downward + downward_prev])
    zero_one = jnp.zeros((1,), jnp.float32)
    tau = jnp.concatenate([zero_one, temporal_weight, zero_one])

    pixel = (dates, lines, width)
    rows = (dates, width)
    ends_shape = (16, LANES)
    vector = (8, LANES)
    window_shape = (blocks - 1, length, lines, width)

    precond, p_first, p_second, p_ends, p_windows, dot_1 = call(
        functools.partial(first_kernel, blocks),
        [pixel, rows, rows, ends_shape, window_shape, vector],
        [pixel],
        [place],
        [obs_mask, precision, observed, rhs_other, inverse],
    )
    p_halo_1, p_halo_2 = swap_rows(p_first, p_second)
    p_left, p_right = swap_ends(p_ends)
    mapped, m_first, m_second, m_ends, m_windows, m_edges, data_weight, dot_2, dot_3 = call(
        functools.partial(second_kernel, blocks),
        [pixel, rows, rows, ends_shape, window_shape, (blocks - 1, 2 * dates_here, width), pixel, vector, vector],
        [pixel, vector],
        [place, tau],
        [weights, precond, p_halo_1, p_halo_2, p_left, p_right, obs_mask, precision, weight_other, inverse],
    )
    m_halo_1, m_halo_2 = swap_rows(m_first, m_second)
    m_left, m_right = swap_ends(m_ends)
    (sums,) = call(
        third_kernel,
        [vector],
        [vector],
        [place, tau],
        [weights, mapped, m_halo_1, m_halo_2, m_left, m_right, data_weight, dot_1, dot_2, dot_3],
    )
    edges_other = send(m_edges)
    precond_other = send(p_windows)
    mapped_other = send(m_windows)
    steps = 1
    while steps < slabs:
        sums = sums + lax.ppermute(sums, "rows", [(i, i ^ steps) for i in range(slabs)])
        steps *= 2
    steps = 1
    while steps < blocks:
        sums = sums + lax.ppermute(sums, "dates", [(i, i ^ steps) for i in range(blocks)])
        steps *= 2

    start = window_start(date_block, dates_here, length, dates)
    own_dates = lax.dynamic_slice_in_dim(precond_other, date_block * dates_here - start, dates_here, 1)
    top, bottom = own_dates[:, :, 0], own_dates[:, :, 7]
    p_edge_1 = jnp.where(parity == 0, bottom, top)
    p_edge_2 = jnp.where(parity == 0, top, bottom)
    other_1, other_2 = swap_rows(
        jnp.concatenate([p_edge_1, edges_other[:, :dates_here]], axis=1),
        jnp.concatenate([p_edge_2, edges_other[:, dates_here:]], axis=1),
    )
    out = (dates_here, lines, all_columns)
    return tuple(
        call(
            functools.partial(last_kernel, blocks),
            [out, out],
            [(length, lines, all_columns), (dates_here, all_columns), (dates_here, all_columns)],
            [place, tau],
            [
                weights, sums, precond, mapped, precond_other, mapped_other, p_halo_1, p_halo_2, m_halo_1, m_halo_2,
                other_1, other_2, obs_mask, precision, observed,
            ],
        )
    )


def solution(mesh):
    return jax.shard_map(
        functools.partial(body, mesh.shape["dates"], mesh.shape["rows"]),
        mesh=mesh,
        in_specs=(
            P("dates", "rows", None),
            P("dates", "rows", None),
            P("dates", "rows", None),
            P(None, "rows", None),
            P(),
            P(None, None, "rows", "dates"),
        ),
        out_specs=(P("dates", "rows", None), P("dates", "rows", None)),
        check_vma=False,
    )
```

```python
import functools

import jax
import jax.numpy as jnp
from jax import lax
from jax.experimental import pallas as pl
from jax.experimental.pallas import tpu as pltpu
from jax.sharding import PartitionSpec as P

MASS = 0.1
LANES = 128
VMEM = pl.BlockSpec(memory_space=pltpu.VMEM)
SMEM = pl.BlockSpec(memory_space=pltpu.SMEM)
HBM = pl.BlockSpec(memory_space=pltpu.HBM)
PARAMS = pltpu.CompilerParams(vmem_limit_bytes=8 * 1024 * 1024)

COST = pl.CostEstimate(flops=1, bytes_accessed=1, transcendentals=0)


def call(kernel, out_shapes, scratch, scalars, arrays, space=VMEM):
    def typed(entry):
        return entry if isinstance(entry[-1], (jnp.dtype, type)) else (entry, jnp.float32)

    if space is HBM:
        arrays = [pltpu.with_memory_space_constraint(array, pltpu.HBM) for array in arrays]
    return pl.pallas_call(
        kernel,
        out_shape=[jax.ShapeDtypeStruct(*typed(entry)) for entry in out_shapes],
        in_specs=[SMEM] * len(scalars) + [space] * len(arrays),
        out_specs=[VMEM] * len(out_shapes),
        scratch_shapes=[pltpu.VMEM(*typed(entry)) if isinstance(entry, tuple) else entry for entry in scratch],
        compiler_params=PARAMS,
        cost_estimate=COST,
    )(*scalars, *arrays)


def tile(index):
    return pl.ds(pl.multiple_of(index * LANES, LANES), LANES)


def columns(block, width):
    return pl.ds(pl.multiple_of(block * width, LANES), width)


def row_ids(width):
    return lax.broadcasted_iota(jnp.int32, (8, width), 0)


def lane_ids(width):
    return lax.broadcasted_iota(jnp.int32, (8, width), 1)


def window_start(block, dates_here, length, dates):
    return jnp.clip(block * dates_here - 1, 0, dates - length)


def edge_rows(value, parity):
    top, bottom = value[0:1], value[7:8]
    return jnp.where(parity == 0, bottom, top), jnp.where(parity == 0, top, bottom)


def halo_rows(first, second, parity):
    above = jnp.where(parity == 0, second, first)
    below = jnp.where(parity == 0, first, second)
    return above, below


def stencil(value, above, below, left, right, later, earlier, weights, diagonal, tau_up, tau_down):
    across, across_prev, downward, downward_prev = weights
    width = value.shape[1]
    rows, lanes = row_ids(width), lane_ids(width)
    next_column = jnp.where(lanes == width - 1, right, pltpu.roll(value, width - 1, 1))
    prev_column = jnp.where(lanes == 0, left, pltpu.roll(value, 1, 1))
    next_row = jnp.where(rows == 7, below, pltpu.roll(value, 7, 0))
    prev_row = jnp.where(rows == 0, above, pltpu.roll(value, 1, 0))
    away = across * next_column + across_prev * prev_column
    away = away + downward * next_row + downward_prev * prev_row
    return diagonal * value - (away + tau_up * later + tau_down * earlier)


def apply_inverse(inverse, source, store, first_total):
    dates = inverse.shape[0]

    def step(index, total):
        lanes = tile(index)
        values = [source[s, :, lanes] for s in range(dates)]
        for t in range(dates):
            mapped = inverse[t, 0, :, lanes].astype(jnp.float32) * values[0]
            for s in range(1, dates):
                mapped = mapped + inverse[t, s, :, lanes].astype(jnp.float32) * values[s]
            total = total + values[t] * mapped
            store(t, lanes, mapped)
        return total

    return lax.fori_loop(0, source.shape[2] // LANES, step, first_total)


def pack_edges(field, parity, first, second, ends):
    dates, _, width = field.shape
    lanes = lane_ids(LANES)
    begin = jnp.zeros((8, LANES), jnp.float32)
    end = begin
    for t in range(dates):
        value = field[t]
        send_1, send_2 = edge_rows(value, parity)
        first[t : t + 1, :] = send_1
        second[t : t + 1, :] = send_2
        begin = jnp.where(lanes == t, value[:, 0:1], begin)
        end = jnp.where(lanes == t, value[:, width - 1 : width], end)
    ends[0:8, :] = begin
    ends[8:16, :] = end


def gather_dates(target, own, received, date_block, blocks, dates_here):
    for j in range(dates_here):
        target[date_block * dates_here + j] = own(j)
    for k in range(1, blocks):
        source = lax.rem(date_block + blocks - k, blocks)
        base = source * dates_here
        for part in received:
            for j in range(part.shape[1]):
                target[base + j] = part[k - 1, j]
            base = base + part.shape[1]


def send_windows(field, parts, date_block, blocks, dates_here):
    length = sum(part.shape[1] for part in parts)
    for k in range(1, blocks):
        target = lax.rem(date_block + k, blocks)
        start = window_start(target, dates_here, length, field.shape[0])
        base = start
        for part in parts:
            for j in range(part.shape[1]):
                part[k - 1, j] = field[base + j]
            base = base + part.shape[1]


def send_kernel(blocks, spans, place, mask, precision, observed, *refs):
    outputs = refs[: len(spans)]
    masks, precisions, observations, arrived = refs[len(spans) :]
    width = masks.shape[3]
    first = min(start for _, start, _ in spans)
    last = max(stop for _, _, stop in spans)
    for k in range(1, blocks):
        there = columns(lax.rem(place[0] + k, blocks), width)

        def copies(j):
            sources = [(mask, masks), (precision, precisions)]
            if any(kind == "rhs" and start <= j < stop for kind, start, stop in spans):
                sources.append((observed, observations))
            return [
                pltpu.make_async_copy(source.at[j, :, there], target.at[k - 1, j], arrived.at[k - 1, j, index])
                for index, (source, target) in enumerate(sources)
            ]

        for j in range(first, last):
            for copy in copies(j):
                copy.start()
        for j in range(first, last):
            for copy in copies(j):
                copy.wait()
            value = masks[k - 1, j].astype(jnp.float32) * precisions[k - 1, j]
            for (kind, start, stop), output in zip(spans, outputs):
                if start <= j < stop:
                    output[k - 1, j - start] = value * observations[k - 1, j] if kind == "rhs" else value


def stage_kernel(
    mask, precision, observed, edge_class, inverse, staged, weight, rhs, weights, last_row, masks, precisions, observations, classes, arrived, loaded
):
    dates_here = mask.shape[0]
    dates = inverse.shape[0]
    loads = [pltpu.make_async_copy(edge_class, classes, loaded.at[dates])]
    loads += [pltpu.make_async_copy(inverse.at[t], staged.at[t], loaded.at[t]) for t in range(dates)]
    copies = [
        [
            pltpu.make_async_copy(source.at[j], target.at[j], arrived.at[j, index])
            for index, (source, target) in enumerate(((mask, masks), (precision, precisions), (observed, observations)))
        ]
        for j in range(dates_here)
    ]
    for group in copies:
        for copy in group:
            copy.start()
    for load in loads:
        load.start()
    for j, group in enumerate(copies):
        for copy in group:
            copy.wait()
        value = masks[j].astype(jnp.float32) * precisions[j]
        weight[j] = value
        rhs[j] = value * observations[j]
    loads[0].wait()
    width = weights.shape[2]
    lanes = lane_ids(width)
    across = jnp.where(lanes == width - 1, 0.0, 0.25 * (classes[0].astype(jnp.float32) + 1.0))
    weights[0] = across
    weights[1] = jnp.where(lanes == 0, 0.0, pltpu.roll(across, 1, 1))
    downward = 0.25 * (classes[1].astype(jnp.float32) + 1.0)
    weights[2] = downward
    last_row[...] = jnp.broadcast_to(downward[7:8], downward.shape)
    for load in loads[1:]:
        load.wait()


def forward_halos(halo_1, halo_2, forwarded, date_block, blocks):
    dates_here = forwarded.shape[1] // 2
    for k in range(1, blocks):
        target = lax.rem(date_block + k, blocks)
        for j in range(dates_here):
            date = pl.ds(target * dates_here + j, 1)
            forwarded[k - 1, j : j + 1, :] = halo_1[date, :]
            forwarded[k - 1, dates_here + j : dates_here + j + 1, :] = halo_2[date, :]


def first_kernel(blocks, place, rhs_here, early, late, inverse, precond, first, second, ends, early_windows, late_windows, dot, rhs):
    date_block, parity = place[0], place[1]
    dates_here = rhs_here.shape[0]
    here = columns(date_block, rhs.shape[2])
    gather_dates(rhs, lambda j: rhs_here[j, :, here], (early, late), date_block, blocks, dates_here)

    def store(t, lanes, value):
        precond[t, :, lanes] = value

    dot[...] = apply_inverse(inverse, rhs, store, jnp.zeros((8, LANES), jnp.float32))
    pack_edges(precond, parity, first, second, ends)
    send_windows(precond, (early_windows, late_windows), date_block, blocks, dates_here)


def edge_weights(place, weights_all, above, lanes):
    across, across_prev, downward = [weights_all[k, :, lanes] for k in range(3)]
    width = across.shape[1]
    rows = row_ids(width)
    downward = jnp.where((rows == 7) & (place[3] == 1), 0.0, downward)
    downward_prev = jnp.where(rows == 0, above[0:1, lanes], pltpu.roll(downward, 1, 0))
    weights = (across, across_prev, downward, downward_prev)
    return weights, MASS + across + across_prev + downward + downward_prev


def pixel_image(place, tau, weights_all, row_above, field, halo_1, halo_2, ends_left, ends_right, data_weight, use):
    date_block, parity = place[0], place[1]
    dates, _, width = field.shape
    here = columns(date_block, width)
    weights, weight_sum = edge_weights(place, weights_all, row_above, here)
    for t in range(dates):
        above, below = halo_rows(halo_1[t : t + 1, :], halo_2[t : t + 1, :], parity)
        tau_up, tau_down = tau[t + 1], tau[t]
        value = field[t]
        diagonal = weight_sum + data_weight[t] + (tau_up + tau_down)
        image = stencil(
            value,
            above,
            below,
            0.0 if ends_left is None else ends_left[:, t : t + 1],
            0.0 if ends_right is None else ends_right[:, t : t + 1],
            field[min(t + 1, dates - 1)],
            field[max(t - 1, 0)],
            weights,
            diagonal,
            tau_up,
            tau_down,
        )
        use(t, value, image)


def fold(value):
    total = value[:, :LANES]
    for index in range(1, value.shape[1] // LANES):
        total = total + value[:, index * LANES : (index + 1) * LANES]
    return total


def second_kernel(
    blocks, place, tau, weights, row_above, precond, halo_1, halo_2, ends_left, ends_right, weight_here, received, inverse,
    mapped, first, second, ends, windows, forwarded, data_weight, dot_image, dot_mapped, image_all, total,
):
    date_block, parity = place[0], place[1]
    dates_here = weight_here.shape[0]
    here = columns(date_block, precond.shape[2])
    gather_dates(data_weight, lambda j: weight_here[j, :, here], (received,), date_block, blocks, dates_here)
    total[...] = jnp.zeros_like(total)

    def use(t, value, image):
        image_all[t] = image
        total[...] = total[...] + fold(value * image)

    pixel_image(place, tau, weights, row_above, precond, halo_1, halo_2, ends_left, ends_right, data_weight, use)
    dot_image[...] = total[...]

    def store(t, lanes, value):
        mapped[t, :, lanes] = value

    dot_mapped[...] = apply_inverse(inverse, image_all, store, jnp.zeros((8, LANES), jnp.float32))
    pack_edges(mapped, parity, first, second, ends)
    send_windows(mapped, (windows,), date_block, blocks, dates_here)
    forward_halos(halo_1, halo_2, forwarded, date_block, blocks)


def third_kernel(
    blocks, place, tau, weights, row_above, mapped, halo_1, halo_2, data_weight, dot_1, dot_2, dot_3, *refs,
):
    *ends, sums, forwarded, total = refs
    left, right = ends or (None, None)
    total[...] = jnp.zeros_like(total)

    def use(t, value, image):
        total[...] = total[...] + fold(value * image)

    pixel_image(place, tau, weights, row_above, mapped, halo_1, halo_2, left, right, data_weight, use)
    rows = row_ids(LANES)
    result = jnp.zeros((8, LANES), jnp.float32)
    for index, dot in enumerate((dot_1, dot_2, dot_3, total)):
        result = jnp.where(rows == index, jnp.sum(dot[...]), result)
    sums[...] = result
    forward_halos(halo_1, halo_2, forwarded, place[0], blocks)


def join_kernel(place, weights, ends, sums, ends_other, sums_other, joined):
    width = weights.shape[2] // 2
    boundary = weights[0, :, width - LANES : width][:, LANES - 1 : LANES]
    dates = jnp.where(place[0] == 0, ends[8:16, :] * ends_other[0:8, :], ends[0:8, :] * ends_other[8:16, :])
    crossing = -2.0 * jnp.sum(boundary * dates)
    joined[...] = sums[...] + sums_other[...] + jnp.where(row_ids(LANES) == 3, crossing, 0.0)


def last_kernel(
    blocks, place, tau, weights_all, row_above, sums, precond, mapped, precond_early, precond_late, mapped_other, own_p1, own_p2, own_m1, own_m2,
    precond_halos, mapped_halos, weight_here, rhs, solution, residual, field, above_all, below_all,
):
    date_block, parity = place[0], place[1]
    dates, _, width = precond.shape
    dates_here, _, all_columns = rhs.shape
    length = field.shape[0]
    one = sums[0:1, :]
    two = sums[1:2, :]
    three = sums[2:3, :]
    four = sums[3:4, :]
    alpha = one / two
    rz = alpha * alpha * three - one
    ahead = 1.0 + rz / one
    curve = ahead * ahead * two - 2.0 * ahead * alpha * three + alpha * alpha * four
    alpha_last = rz / curve
    scale_p = jnp.tile(alpha + alpha_last * ahead, (1, width // LANES))
    scale_m = jnp.tile(-alpha_last * alpha, (1, width // LANES))

    def mix(p, m):
        return scale_p * p + scale_m * m

    start = window_start(date_block, dates_here, length, dates)
    offset = date_block * dates_here - start
    here = columns(date_block, width)
    for j in range(length):
        field[j, :, here] = mix(precond[start + j], mapped[start + j])
    for j in range(dates_here):
        date = pl.ds(date_block * dates_here + j, 1)
        above, below = halo_rows(mix(own_p1[date, :], own_m1[date, :]), mix(own_p2[date, :], own_m2[date, :]), parity)
        above_all[j : j + 1, here] = above
        below_all[j : j + 1, here] = below
    for k in range(1, blocks):
        there = columns(lax.rem(date_block + blocks - k, blocks), width)
        for j in range(length):
            count = precond_early.shape[1]
            other = precond_early[k - 1, j] if j < count else precond_late[k - 1, j - count]
            field[j, :, there] = mix(other, mapped_other[k - 1, j])
        for j in range(dates_here):
            one, two = slice(j, j + 1), slice(dates_here + j, dates_here + j + 1)
            above, below = halo_rows(
                mix(precond_halos[k - 1, one, :], mapped_halos[k - 1, one, :]),
                mix(precond_halos[k - 1, two, :], mapped_halos[k - 1, two, :]),
                parity,
            )
            above_all[j : j + 1, there] = above
            below_all[j : j + 1, there] = below
    weights, weight_sum = edge_weights(place, weights_all, row_above, slice(None))
    for j in range(dates_here):
        tau_up, tau_down = tau[date_block * dates_here + j + 1], tau[date_block * dates_here + j]
        data_weight = weight_here[j]
        place_j = offset + j
        value = field[place_j]
        image = stencil(
            value,
            above_all[j : j + 1, :],
            below_all[j : j + 1, :],
            0.0,
            0.0,
            field[jnp.minimum(place_j + 1, length - 1)],
            field[jnp.maximum(place_j - 1, 0)],
            weights,
            weight_sum + data_weight + (tau_up + tau_down),
            tau_up,
            tau_down,
        )
        solution[j] = value
        residual[j] = rhs[j] - image


def body(blocks, slabs, obs_mask, precision, observed, edge_class, temporal_weight, inverse):
    dates_here, lines, all_columns = observed.shape
    dates = inverse.shape[0]
    width = all_columns // blocks
    length = min(dates_here + (1 if blocks == 2 else 2), dates)
    line_block = lax.axis_index("rows")
    date_block = lax.axis_index("dates")
    parity = lax.rem(line_block, 2)
    at_end = (line_block == slabs - 1).astype(jnp.int32)
    place = jnp.stack([date_block, parity, line_block, at_end]).astype(jnp.int32)

    pairs = [(i, i ^ 1) for i in range(slabs)]
    across_pairs = [(i, i + 1) for i in range(1, slabs - 1, 2)]
    across_pairs = across_pairs + [(b, a) for a, b in across_pairs]

    def rotate(value, k):
        return lax.ppermute(value, "dates", [(i, (i + k) % blocks) for i in range(blocks)])

    def swap_rows(first, second):
        return lax.ppermute(first, "rows", pairs), lax.ppermute(second, "rows", across_pairs)

    def swap_ends(ends):
        if blocks == 2:
            other = rotate(ends, 1)
            return other[8:16], other[0:8]
        forward = [(i, i + 1) for i in range(blocks - 1)]
        backward = [(b, a) for a, b in forward]
        return lax.ppermute(ends[8:16], "dates", forward), lax.ppermute(ends[0:8], "dates", backward)

    def send(stack):
        return jnp.stack([rotate(stack[k - 1], k) for k in range(1, blocks)])

    pixel = (dates, lines, width)
    block = (dates_here, lines, all_columns)
    part = (blocks - 1, dates_here, lines, width)
    rows = (dates, width)
    ends_shape = (16, LANES)
    vector = (8, LANES)
    window_shape = (blocks - 1, length, lines, width)
    edges_shape = (blocks - 1, 2 * dates_here, width)

    half = max(dates_here // 2, 1)

    def send_parts(spans):
        return call(
            functools.partial(send_kernel, blocks, spans),
            [(blocks - 1, stop - start, lines, width) for _, start, stop in spans],
            [(part, jnp.int32), part, part, pltpu.SemaphoreType.DMA((blocks - 1, dates_here, 3))],
            [place],
            [obs_mask, precision, observed],
            HBM,
        )

    (rhs_part,) = send_parts([("rhs", 0, half)])
    rhs_late_part, weight_part = send_parts([("rhs", half, dates_here), ("weight", 0, dates_here)])
    rhs_other = send(rhs_part)
    rhs_late = send(rhs_late_part)
    weight_other = send(weight_part)


    staged, weight_here, rhs_here, weights, last_row = call(
        stage_kernel,
        [(inverse.shape, inverse.dtype), block, block, (3, lines, all_columns), (lines, all_columns)],
        [
            (block, jnp.int32), block, block, (edge_class.shape, jnp.int32),
            pltpu.SemaphoreType.DMA((dates_here, 3)), pltpu.SemaphoreType.DMA((dates + 1,)),
        ],
        [],
        [obs_mask, precision, observed, edge_class, inverse],
        HBM,
    )
    zero_one = jnp.zeros((1,), jnp.float32)
    tau = jnp.concatenate([zero_one, temporal_weight, zero_one])

    row_above = lax.ppermute(last_row, "rows", [(i, i + 1) for i in range(slabs - 1)])
    rhs_here, row_above = lax.optimization_barrier((rhs_here, row_above))
    early_shape = (blocks - 1, (length + 1) // 2, lines, width)
    late_shape = (blocks - 1, length // 2, lines, width)
    precond, p_first, p_second, p_ends, p_early, p_late, dot_1 = call(
        functools.partial(first_kernel, blocks),
        [pixel, rows, rows, ends_shape, early_shape, late_shape, vector],
        [pixel],
        [place],
        [rhs_here, rhs_other, rhs_late, staged],
    )
    p_halo_1, p_halo_2 = swap_rows(p_first, p_second)
    p_left, p_right = swap_ends(p_ends)
    p_early, p_late, p_left, p_halo_2 = lax.optimization_barrier((p_early, p_late, p_left, p_halo_2))
    precond_early = send(p_early)
    precond_late = send(p_late)
    mapped, m_first, m_second, m_ends, m_windows, p_forward, data_weight, dot_2, dot_3 = call(
        functools.partial(second_kernel, blocks),
        [pixel, rows, rows, ends_shape, window_shape, edges_shape, pixel, vector, vector],
        [pixel, vector],
        [place, tau],
        [weights, row_above, precond, p_halo_1, p_halo_2, p_left, p_right, weight_here, weight_other, staged],
    )
    m_halo_1, m_halo_2 = swap_rows(m_first, m_second)
    m_halo_1, precond_early, precond_late = lax.optimization_barrier((m_halo_1, precond_early, precond_late))
    m_ends_other = () if blocks == 2 else swap_ends(m_ends)
    sums, m_forward = call(
        functools.partial(third_kernel, blocks),
        [vector, edges_shape],
        [vector],
        [place, tau],
        [weights, row_above, mapped, m_halo_1, m_halo_2, data_weight, dot_1, dot_2, dot_3, *m_ends_other],
    )
    precond_halos = send(p_forward)
    sums, precond_halos = lax.optimization_barrier((sums, precond_halos))
    if blocks == 2:
        ends_other, sums_other = rotate(m_ends, 1), rotate(sums, 1)
        (sums,) = call(join_kernel, [vector], [], [place], [weights, m_ends, sums, ends_other, sums_other])
    else:
        steps = 1
        while steps < blocks:
            sums = sums + lax.ppermute(sums, "dates", [(i, i ^ steps) for i in range(blocks)])
            steps *= 2
    m_windows, m_forward, sums = lax.optimization_barrier((m_windows, m_forward, sums))
    mapped_halos = send(m_forward)
    mapped_other = send(m_windows)
    steps = 1
    while steps < slabs:
        sums = sums + lax.ppermute(sums, "rows", [(i, i ^ steps) for i in range(slabs)])
        steps *= 2
    return tuple(
        call(
            functools.partial(last_kernel, blocks),
            [block, block],
            [(length, lines, all_columns), (dates_here, all_columns), (dates_here, all_columns)],
            [place, tau],
            [
                weights, row_above, sums, precond, mapped, precond_early, precond_late, mapped_other, p_halo_1, p_halo_2, m_halo_1, m_halo_2,
                precond_halos, mapped_halos, weight_here, rhs_here,
            ],
        )
    )


def solution(mesh):
    return jax.shard_map(
        functools.partial(body, mesh.shape["dates"], mesh.shape["rows"]),
        mesh=mesh,
        in_specs=(
            P("dates", "rows", None),
            P("dates", "rows", None),
            P("dates", "rows", None),
            P(None, "rows", None),
            P(),
            P(None, None, "rows", "dates"),
        ),
        out_specs=(P("dates", "rows", None), P("dates", "rows", None)),
        check_vma=False,
    )
```

```python
import functools

import jax
import jax.numpy as jnp
from jax import lax
from jax.experimental import pallas as pl
from jax.experimental.pallas import tpu as pltpu
from jax.sharding import PartitionSpec as P

MASS = 0.1
LANES = 128
VMEM = pl.BlockSpec(memory_space=pltpu.VMEM)
SMEM = pl.BlockSpec(memory_space=pltpu.SMEM)
HBM = pl.BlockSpec(memory_space=pltpu.HBM)
PARAMS = pltpu.CompilerParams(vmem_limit_bytes=8 * 1024 * 1024)

COST = pl.CostEstimate(flops=1, bytes_accessed=1, transcendentals=0)


def call(kernel, out_shapes, scratch, scalars, arrays, space=VMEM, out_space=VMEM):
    def typed(entry):
        return entry if isinstance(entry[-1], (jnp.dtype, type)) else (entry, jnp.float32)

    if space is HBM:
        arrays = [pltpu.with_memory_space_constraint(array, pltpu.HBM) for array in arrays]
    return pl.pallas_call(
        kernel,
        out_shape=[jax.ShapeDtypeStruct(*typed(entry)) for entry in out_shapes],
        in_specs=[SMEM] * len(scalars) + [space] * len(arrays),
        out_specs=[out_space] * len(out_shapes),
        scratch_shapes=[pltpu.VMEM(*typed(entry)) if isinstance(entry, tuple) else entry for entry in scratch],
        compiler_params=PARAMS,
        cost_estimate=COST,
    )(*scalars, *arrays)


def tile(index, width=LANES):
    return pl.ds(pl.multiple_of(index * width, LANES), width)


def columns(block, width):
    return pl.ds(pl.multiple_of(block * width, LANES), width)


def row_ids(width):
    return lax.broadcasted_iota(jnp.int32, (8, width), 0)


def lane_ids(width):
    return lax.broadcasted_iota(jnp.int32, (8, width), 1)


def window_start(block, dates_here, length, dates):
    return jnp.clip(block * dates_here - 1, 0, dates - length)


def edge_rows(value, parity):
    top, bottom = value[0:1], value[7:8]
    return jnp.where(parity == 0, bottom, top), jnp.where(parity == 0, top, bottom)


def halo_rows(first, second, parity):
    above = jnp.where(parity == 0, second, first)
    below = jnp.where(parity == 0, first, second)
    return above, below


def stencil(value, above, below, left, right, later, earlier, weights, diagonal, tau_up, tau_down):
    across, across_prev, downward, downward_prev = weights
    width = value.shape[1]
    rows, lanes = row_ids(width), lane_ids(width)
    next_column = jnp.where(lanes == width - 1, right, pltpu.roll(value, width - 1, 1))
    prev_column = jnp.where(lanes == 0, left, pltpu.roll(value, 1, 1))
    next_row = jnp.where(rows == 7, below, pltpu.roll(value, 7, 0))
    prev_row = jnp.where(rows == 0, above, pltpu.roll(value, 1, 0))
    away = across * next_column + across_prev * prev_column
    away = away + downward * next_row + downward_prev * prev_row
    return diagonal * value - (away + tau_up * later + tau_down * earlier)


def apply_inverse(inverse, source, store):
    dates = inverse.shape[0]
    width = source.shape[2]
    step_width = 2 * LANES if width % (2 * LANES) == 0 else LANES

    def step(index, total):
        lanes = tile(index, step_width)
        values = [source[s, :, lanes] for s in range(dates)]
        for t in range(dates):
            mapped = inverse[t, 0, :, lanes].astype(jnp.float32) * values[0]
            for s in range(1, dates):
                mapped = mapped + inverse[t, s, :, lanes].astype(jnp.float32) * values[s]
            total = total + values[t] * mapped
            store(t, lanes, mapped)
        return total

    return fold(lax.fori_loop(0, width // step_width, step, jnp.zeros((8, step_width), jnp.float32)))


def pack_edges(field, parity, first, second, ends):
    dates, _, width = field.shape
    lanes = lane_ids(LANES)
    begin = jnp.zeros((8, LANES), jnp.float32)
    end = begin
    for t in range(dates):
        value = field[t]
        send_1, send_2 = edge_rows(value, parity)
        first[t : t + 1, :] = send_1
        second[t : t + 1, :] = send_2
        begin = jnp.where(lanes == t, value[:, 0:1], begin)
        end = jnp.where(lanes == t, value[:, width - 1 : width], end)
    ends[0:8, :] = begin
    ends[8:16, :] = end


def gather_dates(target, own, received, date_block, blocks, dates_here):
    for j in range(dates_here):
        target[date_block * dates_here + j] = own(j)
    for k in range(1, blocks):
        source = lax.rem(date_block + blocks - k, blocks)
        base = source * dates_here
        for part in received:
            for j in range(part.shape[1]):
                target[base + j] = part[k - 1, j]
            base = base + part.shape[1]


def send_windows(field, parts, date_block, blocks, dates_here):
    length = sum(part.shape[1] for part in parts)
    for k in range(1, blocks):
        target = lax.rem(date_block + k, blocks)
        start = window_start(target, dates_here, length, field.shape[0])
        base = start
        for part in parts:
            for j in range(part.shape[1]):
                part[k - 1, j] = field[base + j]
            base = base + part.shape[1]


def send_kernel(blocks, spans, place, mask, precision, observed, *refs):
    outputs = refs[: len(spans)]
    masks, precisions, observations, arrived = refs[len(spans) :]
    width = masks.shape[3]
    first = min(start for _, start, _ in spans)
    last = max(stop for _, _, stop in spans)
    for k in range(1, blocks):
        there = columns(lax.rem(place[0] + k, blocks), width)

        def copies(j):
            sources = [(mask, masks), (precision, precisions)]
            if any(kind == "rhs" and start <= j < stop for kind, start, stop in spans):
                sources.append((observed, observations))
            return [
                pltpu.make_async_copy(source.at[j, :, there], target.at[k - 1, j], arrived.at[k - 1, j, index])
                for index, (source, target) in enumerate(sources)
            ]

        for j in range(first, last):
            for copy in copies(j):
                copy.start()
        for j in range(first, last):
            for copy in copies(j):
                copy.wait()
            value = masks[k - 1, j].astype(jnp.float32) * precisions[k - 1, j]
            for (kind, start, stop), output in zip(spans, outputs):
                if start <= j < stop:
                    output[k - 1, j - start] = value * observations[k - 1, j] if kind == "rhs" else value


def stage_kernel(
    mask, precision, observed, edge_class, inverse, staged, weight, rhs, weights, last_row, masks, precisions, observations, classes, arrived, loaded
):
    dates_here = mask.shape[0]
    dates = inverse.shape[0]
    loads = [pltpu.make_async_copy(edge_class, classes, loaded.at[dates])]
    loads += [pltpu.make_async_copy(inverse.at[t], staged.at[t], loaded.at[t]) for t in range(dates)]
    copies = [
        [
            pltpu.make_async_copy(source.at[j], target.at[j], arrived.at[j, index])
            for index, (source, target) in enumerate(((mask, masks), (precision, precisions), (observed, observations)))
        ]
        for j in range(dates_here)
    ]
    for group in copies:
        for copy in group:
            copy.start()
    for load in loads:
        load.start()
    for j, group in enumerate(copies):
        for copy in group:
            copy.wait()
        value = masks[j].astype(jnp.float32) * precisions[j]
        weight[j] = value
        rhs[j] = value * observations[j]
    loads[0].wait()
    width = weights.shape[2]
    lanes = lane_ids(width)
    across = jnp.where(lanes == width - 1, 0.0, 0.25 * (classes[0].astype(jnp.float32) + 1.0))
    weights[0] = across
    weights[1] = jnp.where(lanes == 0, 0.0, pltpu.roll(across, 1, 1))
    downward = 0.25 * (classes[1].astype(jnp.float32) + 1.0)
    weights[2] = downward
    last_row[...] = jnp.broadcast_to(downward[7:8], downward.shape)
    for load in loads[1:]:
        load.wait()


def forward_halos(halo_1, halo_2, forwarded, date_block, blocks):
    dates_here = forwarded.shape[1] // 2
    for k in range(1, blocks):
        target = lax.rem(date_block + k, blocks)
        for j in range(dates_here):
            date = pl.ds(target * dates_here + j, 1)
            forwarded[k - 1, j : j + 1, :] = halo_1[date, :]
            forwarded[k - 1, dates_here + j : dates_here + j + 1, :] = halo_2[date, :]


def first_kernel(blocks, place, rhs_here, early, late, inverse, precond, first, second, ends, early_windows, late_windows, dot, rhs):
    date_block, parity = place[0], place[1]
    dates_here = rhs_here.shape[0]
    here = columns(date_block, rhs.shape[2])
    gather_dates(rhs, lambda j: rhs_here[j, :, here], (early, late), date_block, blocks, dates_here)

    def store(t, lanes, value):
        precond[t, :, lanes] = value

    dot[...] = apply_inverse(inverse, rhs, store)
    pack_edges(precond, parity, first, second, ends)
    send_windows(precond, (early_windows, late_windows), date_block, blocks, dates_here)


def edge_weights(place, weights_all, above, lanes):
    across, across_prev, downward = [weights_all[k, :, lanes] for k in range(3)]
    width = across.shape[1]
    rows = row_ids(width)
    downward = jnp.where((rows == 7) & (place[3] == 1), 0.0, downward)
    row_above = jnp.where(place[2] == 0, 0.0, above[0:1, lanes])
    downward_prev = jnp.where(rows == 0, row_above, pltpu.roll(downward, 1, 0))
    weights = (across, across_prev, downward, downward_prev)
    return weights, MASS + across + across_prev + downward + downward_prev


def pixel_image(place, tau, weights_all, row_above, field, halo_1, halo_2, ends_left, ends_right, data_weight, use):
    date_block, parity = place[0], place[1]
    dates, _, width = field.shape
    here = columns(date_block, width)
    weights, weight_sum = edge_weights(place, weights_all, row_above, here)
    for t in range(dates):
        above, below = halo_rows(halo_1[t : t + 1, :], halo_2[t : t + 1, :], parity)
        tau_up, tau_down = tau[t + 1], tau[t]
        value = field[t]
        diagonal = weight_sum + data_weight[t] + (tau_up + tau_down)
        image = stencil(
            value,
            above,
            below,
            0.0 if ends_left is None else ends_left[:, t : t + 1],
            0.0 if ends_right is None else ends_right[:, t : t + 1],
            field[min(t + 1, dates - 1)],
            field[max(t - 1, 0)],
            weights,
            diagonal,
            tau_up,
            tau_down,
        )
        use(t, value, image)


def fold(value):
    total = value[:, :LANES]
    for index in range(1, value.shape[1] // LANES):
        total = total + value[:, index * LANES : (index + 1) * LANES]
    return total


def second_kernel(
    blocks, place, tau, weights, row_above, precond, halo_1, halo_2, ends_left, ends_right, weight_here, received, inverse,
    mapped, first, second, ends, windows, forwarded, data_weight, dot_image, dot_mapped, image_all, total,
):
    date_block, parity = place[0], place[1]
    dates_here = weight_here.shape[0]
    here = columns(date_block, precond.shape[2])
    gather_dates(data_weight, lambda j: weight_here[j, :, here], (received,), date_block, blocks, dates_here)
    total[...] = jnp.zeros_like(total)

    def use(t, value, image):
        image_all[t] = image
        total[...] = total[...] + fold(value * image)

    pixel_image(place, tau, weights, row_above, precond, halo_1, halo_2, ends_left, ends_right, data_weight, use)
    dot_image[...] = total[...]

    def store(t, lanes, value):
        mapped[t, :, lanes] = value

    dot_mapped[...] = apply_inverse(inverse, image_all, store)
    pack_edges(mapped, parity, first, second, ends)
    send_windows(mapped, (windows,), date_block, blocks, dates_here)
    forward_halos(halo_1, halo_2, forwarded, date_block, blocks)


def third_kernel(
    blocks, place, tau, weights, row_above, mapped, halo_1, halo_2, data_weight, dot_1, dot_2, dot_3, *refs,
):
    *ends, sums, forwarded, total = refs
    left, right = ends or (None, None)
    total[...] = jnp.zeros_like(total)

    def use(t, value, image):
        total[...] = total[...] + fold(value * image)

    pixel_image(place, tau, weights, row_above, mapped, halo_1, halo_2, left, right, data_weight, use)
    rows = row_ids(LANES)
    result = jnp.zeros((8, LANES), jnp.float32)
    for index, dot in enumerate((dot_1, dot_2, dot_3, total)):
        result = jnp.where(rows == index, jnp.sum(dot[...]), result)
    sums[...] = result
    forward_halos(halo_1, halo_2, forwarded, place[0], blocks)


def join_kernel(place, weights, ends, sums, ends_other, sums_other, joined):
    width = weights.shape[2] // 2
    boundary = weights[0, :, width - LANES : width][:, LANES - 1 : LANES]
    dates = jnp.where(place[0] == 0, ends[8:16, :] * ends_other[0:8, :], ends[0:8, :] * ends_other[8:16, :])
    crossing = -2.0 * jnp.sum(boundary * dates)
    joined[...] = sums[...] + sums_other[...] + jnp.where(row_ids(LANES) == 3, crossing, 0.0)


def last_kernel(
    blocks, place, tau, weights_all, row_above, sums, precond, mapped, precond_early, precond_late, mapped_other, own_p1, own_p2, own_m1, own_m2,
    precond_halos, mapped_halos, weight_here, rhs, solution, residual, field, above_all, below_all, remainder, sent,
):
    date_block, parity = place[0], place[1]
    dates, _, width = precond.shape
    dates_here, _, all_columns = rhs.shape
    length = field.shape[0]
    one = sums[0:1, :]
    two = sums[1:2, :]
    three = sums[2:3, :]
    four = sums[3:4, :]
    alpha = one / two
    rz = alpha * alpha * three - one
    ahead = 1.0 + rz / one
    curve = ahead * ahead * two - 2.0 * ahead * alpha * three + alpha * alpha * four
    alpha_last = rz / curve
    scale_p = jnp.tile(alpha + alpha_last * ahead, (1, width // LANES))
    scale_m = jnp.tile(-alpha_last * alpha, (1, width // LANES))

    def mix(p, m):
        return scale_p * p + scale_m * m

    start = window_start(date_block, dates_here, length, dates)
    offset = date_block * dates_here - start
    here = columns(date_block, width)
    for j in range(length):
        field[j, :, here] = mix(precond[start + j], mapped[start + j])
    for j in range(dates_here):
        date = pl.ds(date_block * dates_here + j, 1)
        above, below = halo_rows(mix(own_p1[date, :], own_m1[date, :]), mix(own_p2[date, :], own_m2[date, :]), parity)
        above_all[j : j + 1, here] = above
        below_all[j : j + 1, here] = below
    for k in range(1, blocks):
        there = columns(lax.rem(date_block + blocks - k, blocks), width)
        for j in range(length):
            count = precond_early.shape[1]
            other = precond_early[k - 1, j] if j < count else precond_late[k - 1, j - count]
            field[j, :, there] = mix(other, mapped_other[k - 1, j])
        for j in range(dates_here):
            one, two = slice(j, j + 1), slice(dates_here + j, dates_here + j + 1)
            above, below = halo_rows(
                mix(precond_halos[k - 1, one, :], mapped_halos[k - 1, one, :]),
                mix(precond_halos[k - 1, two, :], mapped_halos[k - 1, two, :]),
                parity,
            )
            above_all[j : j + 1, there] = above
            below_all[j : j + 1, there] = below
    copies = [pltpu.make_async_copy(field.at[offset + j], solution.at[j], sent.at[0, j]) for j in range(dates_here)]
    for copy in copies:
        copy.start()
    weights, weight_sum = edge_weights(place, weights_all, row_above, slice(None))
    for j in range(dates_here):
        tau_up, tau_down = tau[date_block * dates_here + j + 1], tau[date_block * dates_here + j]
        data_weight = weight_here[j]
        place_j = offset + j
        value = field[place_j]
        image = stencil(
            value,
            above_all[j : j + 1, :],
            below_all[j : j + 1, :],
            0.0,
            0.0,
            field[jnp.minimum(place_j + 1, length - 1)],
            field[jnp.maximum(place_j - 1, 0)],
            weights,
            weight_sum + data_weight + (tau_up + tau_down),
            tau_up,
            tau_down,
        )
        remainder[j] = rhs[j] - image
        copy = pltpu.make_async_copy(remainder.at[j], residual.at[j], sent.at[1, j])
        copy.start()
        copies.append(copy)
    for copy in copies:
        copy.wait()


def body(blocks, slabs, obs_mask, precision, observed, edge_class, temporal_weight, inverse):
    dates_here, lines, all_columns = observed.shape
    dates = inverse.shape[0]
    width = all_columns // blocks
    length = min(dates_here + (1 if blocks == 2 else 2), dates)
    line_block = lax.axis_index("rows")
    date_block = lax.axis_index("dates")
    parity = lax.rem(line_block, 2)
    at_end = (line_block == slabs - 1).astype(jnp.int32)
    place = jnp.stack([date_block, parity, line_block, at_end]).astype(jnp.int32)

    pairs = [(i, i ^ 1) for i in range(slabs)]
    across_pairs = [(i, (i + 1) % slabs) for i in range(1, slabs, 2)]
    across_pairs = across_pairs + [(b, a) for a, b in across_pairs]

    def rotate(value, k):
        return lax.ppermute(value, "dates", [(i, (i + k) % blocks) for i in range(blocks)])

    def swap_rows(first, second):
        return lax.ppermute(first, "rows", pairs), lax.ppermute(second, "rows", across_pairs)

    def swap_ends(ends):
        if blocks == 2:
            other = rotate(ends, 1)
            return other[8:16], other[0:8]
        forward = [(i, i + 1) for i in range(blocks - 1)]
        backward = [(b, a) for a, b in forward]
        return lax.ppermute(ends[8:16], "dates", forward), lax.ppermute(ends[0:8], "dates", backward)

    def send(stack):
        return jnp.stack([rotate(stack[k - 1], k) for k in range(1, blocks)])

    pixel = (dates, lines, width)
    block = (dates_here, lines, all_columns)
    part = (blocks - 1, dates_here, lines, width)
    rows = (dates, width)
    ends_shape = (16, LANES)
    vector = (8, LANES)
    window_shape = (blocks - 1, length, lines, width)
    edges_shape = (blocks - 1, 2 * dates_here, width)

    half = max(dates_here // 2, 1)

    def send_parts(spans):
        return call(
            functools.partial(send_kernel, blocks, spans),
            [(blocks - 1, stop - start, lines, width) for _, start, stop in spans],
            [(part, jnp.int32), part, part, pltpu.SemaphoreType.DMA((blocks - 1, dates_here, 3))],
            [place],
            [obs_mask, precision, observed],
            HBM,
        )

    (rhs_part,) = send_parts([("rhs", 0, half)])
    rhs_late_part, weight_part = send_parts([("rhs", half, dates_here), ("weight", 0, dates_here)])
    rhs_other = send(rhs_part)
    rhs_late = send(rhs_late_part)
    weight_other = send(weight_part)


    staged, weight_here, rhs_here, weights, last_row = call(
        stage_kernel,
        [(inverse.shape, inverse.dtype), block, block, (3, lines, all_columns), (lines, all_columns)],
        [
            (block, jnp.int32), block, block, (edge_class.shape, jnp.int32),
            pltpu.SemaphoreType.DMA((dates_here, 3)), pltpu.SemaphoreType.DMA((dates + 1,)),
        ],
        [],
        [obs_mask, precision, observed, edge_class, inverse],
        HBM,
    )
    zero_one = jnp.zeros((1,), jnp.float32)
    tau = jnp.concatenate([zero_one, temporal_weight, zero_one])

    row_above = lax.ppermute(last_row, "rows", [(i, (i + 1) % slabs) for i in range(slabs)])
    rhs_here, row_above = lax.optimization_barrier((rhs_here, row_above))
    early_shape = (blocks - 1, (length + 1) // 2, lines, width)
    late_shape = (blocks - 1, length // 2, lines, width)
    precond, p_first, p_second, p_ends, p_early, p_late, dot_1 = call(
        functools.partial(first_kernel, blocks),
        [pixel, rows, rows, ends_shape, early_shape, late_shape, vector],
        [pixel],
        [place],
        [rhs_here, rhs_other, rhs_late, staged],
    )
    p_halo_1, p_halo_2 = swap_rows(p_first, p_second)
    p_left, p_right = swap_ends(p_ends)
    p_early, p_late, p_left, p_halo_2 = lax.optimization_barrier((p_early, p_late, p_left, p_halo_2))
    precond_early = send(p_early)
    precond_late = send(p_late)
    mapped, m_first, m_second, m_ends, m_windows, p_forward, data_weight, dot_2, dot_3 = call(
        functools.partial(second_kernel, blocks),
        [pixel, rows, rows, ends_shape, window_shape, edges_shape, pixel, vector, vector],
        [pixel, vector],
        [place, tau],
        [weights, row_above, precond, p_halo_1, p_halo_2, p_left, p_right, weight_here, weight_other, staged],
    )
    m_halo_1, m_halo_2 = swap_rows(m_first, m_second)
    m_ends_other = () if blocks == 2 else swap_ends(m_ends)
    sums, m_forward = call(
        functools.partial(third_kernel, blocks),
        [vector, edges_shape],
        [vector],
        [place, tau],
        [weights, row_above, mapped, m_halo_1, m_halo_2, data_weight, dot_1, dot_2, dot_3, *m_ends_other],
    )
    precond_halos = send(p_forward)
    sums, precond_early, precond_late = lax.optimization_barrier((sums, precond_early, precond_late))
    if blocks == 2:
        ends_other, sums_other = rotate(m_ends, 1), rotate(sums, 1)
        (sums,) = call(join_kernel, [vector], [], [place], [weights, m_ends, sums, ends_other, sums_other])
    else:
        steps = 1
        while steps < blocks:
            sums = sums + lax.ppermute(sums, "dates", [(i, i ^ steps) for i in range(blocks)])
            steps *= 2
    m_windows, m_forward, precond_halos, sums = lax.optimization_barrier((m_windows, m_forward, precond_halos, sums))
    mapped_halos = send(m_forward)
    mapped_other = send(m_windows)
    steps = 1
    while steps < slabs:
        sums = sums + lax.ppermute(sums, "rows", [(i, i ^ steps) for i in range(slabs)])
        steps *= 2
    return tuple(
        call(
            functools.partial(last_kernel, blocks),
            [block, block],
            [
                (length, lines, all_columns), (dates_here, all_columns), (dates_here, all_columns), block,
                pltpu.SemaphoreType.DMA((2, dates_here)),
            ],
            [place, tau],
            [
                weights, row_above, sums, precond, mapped, precond_early, precond_late, mapped_other, p_halo_1, p_halo_2, m_halo_1, m_halo_2,
                precond_halos, mapped_halos, weight_here, rhs_here,
            ],
            out_space=HBM,
        )
    )


def solution(mesh):
    return jax.shard_map(
        functools.partial(body, mesh.shape["dates"], mesh.shape["rows"]),
        mesh=mesh,
        in_specs=(
            P("dates", "rows", None),
            P("dates", "rows", None),
            P("dates", "rows", None),
            P(None, "rows", None),
            P(),
            P(None, None, "rows", "dates"),
        ),
        out_specs=(P("dates", "rows", None), P("dates", "rows", None)),
        check_vma=False,
    )
```

```python
import functools

import jax
import jax.numpy as jnp
from jax import lax
from jax.experimental import pallas as pl
from jax.experimental.pallas import tpu as pltpu
from jax.sharding import PartitionSpec as P

MASS = 0.1
LANES = 128
VMEM = pl.BlockSpec(memory_space=pltpu.VMEM)
SMEM = pl.BlockSpec(memory_space=pltpu.SMEM)
HBM = pl.BlockSpec(memory_space=pltpu.HBM)
PARAMS = pltpu.CompilerParams(vmem_limit_bytes=8 * 1024 * 1024)

COST = pl.CostEstimate(flops=1, bytes_accessed=1, transcendentals=0)


def call(kernel, out_shapes, scratch, scalars, arrays, space=VMEM, out_space=VMEM):
    def typed(entry):
        return entry if isinstance(entry[-1], (jnp.dtype, type)) else (entry, jnp.float32)

    if space is HBM:
        arrays = [pltpu.with_memory_space_constraint(array, pltpu.HBM) for array in arrays]
    return pl.pallas_call(
        kernel,
        out_shape=[jax.ShapeDtypeStruct(*typed(entry)) for entry in out_shapes],
        in_specs=[SMEM] * len(scalars) + [space] * len(arrays),
        out_specs=[out_space] * len(out_shapes),
        scratch_shapes=[pltpu.VMEM(*typed(entry)) if isinstance(entry, tuple) else entry for entry in scratch],
        compiler_params=PARAMS,
        cost_estimate=COST,
    )(*scalars, *arrays)


def tile(index, width=LANES):
    return pl.ds(pl.multiple_of(index * width, LANES), width)


def columns(block, width):
    return pl.ds(pl.multiple_of(block * width, LANES), width)


def row_ids(width):
    return lax.broadcasted_iota(jnp.int32, (8, width), 0)


def lane_ids(width):
    return lax.broadcasted_iota(jnp.int32, (8, width), 1)


def window_start(block, dates_here, length, dates):
    return jnp.clip(block * dates_here - 1, 0, dates - length)


def edge_rows(value, parity):
    top, bottom = value[0:1], value[7:8]
    return jnp.where(parity == 0, bottom, top), jnp.where(parity == 0, top, bottom)


def halo_rows(first, second, parity):
    above = jnp.where(parity == 0, second, first)
    below = jnp.where(parity == 0, first, second)
    return above, below


def stencil(value, above, below, left, right, later, earlier, weights, diagonal, tau_up, tau_down):
    across, across_prev, downward, downward_prev = weights
    width = value.shape[1]
    rows, lanes = row_ids(width), lane_ids(width)
    next_column = jnp.where(lanes == width - 1, right, pltpu.roll(value, width - 1, 1))
    prev_column = jnp.where(lanes == 0, left, pltpu.roll(value, 1, 1))
    next_row = jnp.where(rows == 7, below, pltpu.roll(value, 7, 0))
    prev_row = jnp.where(rows == 0, above, pltpu.roll(value, 1, 0))
    away = across * next_column + across_prev * prev_column
    away = away + downward * next_row + downward_prev * prev_row
    return diagonal * value - (away + tau_up * later + tau_down * earlier)


def apply_inverse(inverse, source, store):
    dates = inverse.shape[0]
    width = source.shape[2]
    step_width = 2 * LANES if width % (2 * LANES) == 0 else LANES

    def step(index, total):
        lanes = tile(index, step_width)
        values = [source[s, :, lanes] for s in range(dates)]
        for t in range(dates):
            mapped = inverse[t, 0, :, lanes].astype(jnp.float32) * values[0]
            for s in range(1, dates):
                mapped = mapped + inverse[t, s, :, lanes].astype(jnp.float32) * values[s]
            total = total + values[t] * mapped
            store(t, lanes, mapped)
        return total

    return fold(lax.fori_loop(0, width // step_width, step, jnp.zeros((8, step_width), jnp.float32)))


def pack_edges(field, parity, first, second, ends):
    dates, _, width = field.shape
    lanes = lane_ids(LANES)
    begin = jnp.zeros((8, LANES), jnp.float32)
    end = begin
    for t in range(dates):
        value = field[t]
        send_1, send_2 = edge_rows(value, parity)
        first[t : t + 1, :] = send_1
        second[t : t + 1, :] = send_2
        begin = jnp.where(lanes == t, value[:, 0:1], begin)
        end = jnp.where(lanes == t, value[:, width - 1 : width], end)
    ends[0:8, :] = begin
    ends[8:16, :] = end


def gather_dates(target, own, received, date_block, blocks, dates_here):
    for j in range(dates_here):
        target[date_block * dates_here + j] = own(j)
    for k in range(1, blocks):
        source = lax.rem(date_block + blocks - k, blocks)
        base = source * dates_here
        for part in received:
            for j in range(part.shape[1]):
                target[base + j] = part[k - 1, j]
            base = base + part.shape[1]


def send_windows(field, parts, date_block, blocks, dates_here):
    length = sum(part.shape[1] for part in parts)
    for k in range(1, blocks):
        target = lax.rem(date_block + k, blocks)
        start = window_start(target, dates_here, length, field.shape[0])
        base = start
        for part in parts:
            for j in range(part.shape[1]):
                part[k - 1, j] = field[base + j]
            base = base + part.shape[1]


def send_kernel(blocks, spans, mask, precision, observed, *refs):
    outputs = refs[: len(spans)]
    masks, precisions, observations, arrived = refs[len(spans) :]
    width = masks.shape[3]
    first = min(start for _, start, _ in spans)
    last = max(stop for _, _, stop in spans)
    for k in range(1, blocks):
        there = columns(lax.rem(lax.axis_index("dates") + k, blocks), width)

        def copies(j):
            sources = [(mask, masks), (precision, precisions)]
            if any(kind == "rhs" and start <= j < stop for kind, start, stop in spans):
                sources.append((observed, observations))
            return [
                pltpu.make_async_copy(source.at[j, :, there], target.at[k - 1, j], arrived.at[k - 1, j, index])
                for index, (source, target) in enumerate(sources)
            ]

        for j in range(first, last):
            for copy in copies(j):
                copy.start()
        for j in range(first, last):
            for copy in copies(j):
                copy.wait()
            value = masks[k - 1, j].astype(jnp.float32) * precisions[k - 1, j]
            for (kind, start, stop), output in zip(spans, outputs):
                if start <= j < stop:
                    output[k - 1, j - start] = value * observations[k - 1, j] if kind == "rhs" else value


def stage_kernel(
    mask, precision, observed, edge_class, inverse, staged, weight, rhs, weights, last_row, masks, precisions, observations, classes, arrived, loaded
):
    dates_here = mask.shape[0]
    dates = inverse.shape[0]
    loads = [pltpu.make_async_copy(edge_class, classes, loaded.at[dates])]
    loads += [pltpu.make_async_copy(inverse.at[t], staged.at[t], loaded.at[t]) for t in range(dates)]
    copies = [
        [
            pltpu.make_async_copy(source.at[j], target.at[j], arrived.at[j, index])
            for index, (source, target) in enumerate(((mask, masks), (precision, precisions), (observed, observations)))
        ]
        for j in range(dates_here)
    ]
    for group in copies:
        for copy in group:
            copy.start()
    for load in loads:
        load.start()
    for j, group in enumerate(copies):
        for copy in group:
            copy.wait()
        value = masks[j].astype(jnp.float32) * precisions[j]
        weight[j] = value
        rhs[j] = value * observations[j]
    loads[0].wait()
    width = weights.shape[2]
    lanes = lane_ids(width)
    across = jnp.where(lanes == width - 1, 0.0, 0.25 * (classes[0].astype(jnp.float32) + 1.0))
    weights[0] = across
    weights[1] = jnp.where(lanes == 0, 0.0, pltpu.roll(across, 1, 1))
    downward = 0.25 * (classes[1].astype(jnp.float32) + 1.0)
    weights[2] = downward
    last_row[...] = jnp.broadcast_to(downward[7:8], downward.shape)
    for load in loads[1:]:
        load.wait()


def forward_halos(halo_1, halo_2, forwarded, date_block, blocks):
    dates_here = forwarded.shape[1] // 2
    for k in range(1, blocks):
        target = lax.rem(date_block + k, blocks)
        for j in range(dates_here):
            date = pl.ds(target * dates_here + j, 1)
            forwarded[k - 1, j : j + 1, :] = halo_1[date, :]
            forwarded[k - 1, dates_here + j : dates_here + j + 1, :] = halo_2[date, :]


def first_kernel(blocks, rhs_here, early, late, inverse, precond, first, second, ends, early_windows, late_windows, dot, rhs):
    date_block, parity = lax.axis_index("dates"), lax.rem(lax.axis_index("rows"), 2)
    dates_here = rhs_here.shape[0]
    here = columns(date_block, rhs.shape[2])
    gather_dates(rhs, lambda j: rhs_here[j, :, here], (early, late), date_block, blocks, dates_here)

    def store(t, lanes, value):
        precond[t, :, lanes] = value

    dot[...] = apply_inverse(inverse, rhs, store)
    pack_edges(precond, parity, first, second, ends)
    send_windows(precond, (early_windows, late_windows), date_block, blocks, dates_here)


def edge_weights(weights_all, above, lanes):
    across, across_prev, downward = [weights_all[k, :, lanes] for k in range(3)]
    width = across.shape[1]
    rows = row_ids(width)
    downward = jnp.where((rows == 7) & (lax.axis_index("rows") == lax.axis_size("rows") - 1), 0.0, downward)
    row_above = jnp.where(lax.axis_index("rows") == 0, 0.0, above[0:1, lanes])
    downward_prev = jnp.where(rows == 0, row_above, pltpu.roll(downward, 1, 0))
    weights = (across, across_prev, downward, downward_prev)
    return weights, MASS + across + across_prev + downward + downward_prev


def pixel_image(tau, weights_all, row_above, field, halo_1, halo_2, ends_left, ends_right, data_weight, use):
    date_block, parity = lax.axis_index("dates"), lax.rem(lax.axis_index("rows"), 2)
    dates, _, width = field.shape
    here = columns(date_block, width)
    weights, weight_sum = edge_weights(weights_all, row_above, here)
    for t in range(dates):
        above, below = halo_rows(halo_1[t : t + 1, :], halo_2[t : t + 1, :], parity)
        tau_up, tau_down = spread(tau, t + 1, width), spread(tau, t, width)
        value = field[t]
        diagonal = weight_sum + data_weight[t] + (tau_up + tau_down)
        image = stencil(
            value,
            above,
            below,
            0.0 if ends_left is None else ends_left[:, t : t + 1],
            0.0 if ends_right is None else ends_right[:, t : t + 1],
            field[min(t + 1, dates - 1)],
            field[max(t - 1, 0)],
            weights,
            diagonal,
            tau_up,
            tau_down,
        )
        use(t, value, image)


def spread(tau, index, width):
    return jnp.tile(jnp.broadcast_to(tau[pl.ds(index, 1), :], (8, LANES)), (1, width // LANES))


def fold(value):
    total = value[:, :LANES]
    for index in range(1, value.shape[1] // LANES):
        total = total + value[:, index * LANES : (index + 1) * LANES]
    return total


def second_kernel(
    blocks, tau, weights, row_above, precond, halo_1, halo_2, ends_left, ends_right, weight_here, received, inverse,
    mapped, first, second, ends, windows, forwarded, data_weight, dot_image, dot_mapped, image_all, total,
):
    date_block, parity = lax.axis_index("dates"), lax.rem(lax.axis_index("rows"), 2)
    dates_here = weight_here.shape[0]
    here = columns(date_block, precond.shape[2])
    gather_dates(data_weight, lambda j: weight_here[j, :, here], (received,), date_block, blocks, dates_here)
    total[...] = jnp.zeros_like(total)

    def use(t, value, image):
        image_all[t] = image
        total[...] = total[...] + fold(value * image)

    pixel_image(tau, weights, row_above, precond, halo_1, halo_2, ends_left, ends_right, data_weight, use)
    dot_image[...] = total[...]

    def store(t, lanes, value):
        mapped[t, :, lanes] = value

    dot_mapped[...] = apply_inverse(inverse, image_all, store)
    pack_edges(mapped, parity, first, second, ends)
    send_windows(mapped, (windows,), date_block, blocks, dates_here)
    forward_halos(halo_1, halo_2, forwarded, date_block, blocks)


def third_kernel(
    blocks, tau, weights, row_above, mapped, halo_1, halo_2, data_weight, dot_1, dot_2, dot_3, *refs,
):
    *ends, sums, forwarded, total = refs
    left, right = ends or (None, None)
    total[...] = jnp.zeros_like(total)

    def use(t, value, image):
        total[...] = total[...] + fold(value * image)

    pixel_image(tau, weights, row_above, mapped, halo_1, halo_2, left, right, data_weight, use)
    rows = row_ids(LANES)
    result = jnp.zeros((8, LANES), jnp.float32)
    for index, dot in enumerate((dot_1, dot_2, dot_3, total)):
        result = jnp.where(rows == index, jnp.sum(dot[...]), result)
    sums[...] = result
    forward_halos(halo_1, halo_2, forwarded, lax.axis_index("dates"), blocks)


def join_kernel(weights, ends, sums, ends_other, sums_other, joined):
    width = weights.shape[2] // 2
    boundary = weights[0, :, width - LANES : width][:, LANES - 1 : LANES]
    dates = jnp.where(lax.axis_index("dates") == 0, ends[8:16, :] * ends_other[0:8, :], ends[0:8, :] * ends_other[8:16, :])
    crossing = -2.0 * jnp.sum(boundary * dates)
    joined[...] = sums[...] + sums_other[...] + jnp.where(row_ids(LANES) == 3, crossing, 0.0)


def last_kernel(
    blocks, tau, weights_all, row_above, sums, precond, mapped, precond_early, precond_late, mapped_other, own_p1, own_p2, own_m1, own_m2,
    precond_halos, mapped_halos, weight_here, rhs, solution, residual, field, above_all, below_all, remainder, sent,
):
    date_block, parity = lax.axis_index("dates"), lax.rem(lax.axis_index("rows"), 2)
    dates, _, width = precond.shape
    dates_here, _, all_columns = rhs.shape
    length = field.shape[0]
    one = sums[0:1, :]
    two = sums[1:2, :]
    three = sums[2:3, :]
    four = sums[3:4, :]
    alpha = one / two
    rz = alpha * alpha * three - one
    ahead = 1.0 + rz / one
    curve = ahead * ahead * two - 2.0 * ahead * alpha * three + alpha * alpha * four
    alpha_last = rz / curve
    scale_p = jnp.tile(alpha + alpha_last * ahead, (1, width // LANES))
    scale_m = jnp.tile(-alpha_last * alpha, (1, width // LANES))

    def mix(p, m):
        return scale_p * p + scale_m * m

    start = window_start(date_block, dates_here, length, dates)
    offset = date_block * dates_here - start
    here = columns(date_block, width)
    for j in range(length):
        field[j, :, here] = mix(precond[start + j], mapped[start + j])
    first_date = date_block * dates_here

    def own(rows):
        if dates_here % 8 == 0:
            return rows[pl.ds(pl.multiple_of(first_date, 8), dates_here), :]
        return jnp.concatenate([rows[pl.ds(first_date + j, 1), :] for j in range(dates_here)], axis=0)

    above, below = halo_rows(mix(own(own_p1), own(own_m1)), mix(own(own_p2), own(own_m2)), parity)
    above_all[:, here] = above
    below_all[:, here] = below
    for k in range(1, blocks):
        there = columns(lax.rem(date_block + blocks - k, blocks), width)
        for j in range(length):
            count = precond_early.shape[1]
            other = precond_early[k - 1, j] if j < count else precond_late[k - 1, j - count]
            field[j, :, there] = mix(other, mapped_other[k - 1, j])
        above, below = halo_rows(
            mix(precond_halos[k - 1, :dates_here, :], mapped_halos[k - 1, :dates_here, :]),
            mix(precond_halos[k - 1, dates_here:, :], mapped_halos[k - 1, dates_here:, :]),
            parity,
        )
        above_all[:, there] = above
        below_all[:, there] = below
    copies = [pltpu.make_async_copy(field.at[offset + j], solution.at[j], sent.at[0, j]) for j in range(dates_here)]
    for copy in copies:
        copy.start()
    weights, weight_sum = edge_weights(weights_all, row_above, slice(None))
    for j in range(dates_here):
        date = date_block * dates_here + j
        tau_up, tau_down = spread(tau, date + 1, all_columns), spread(tau, date, all_columns)
        data_weight = weight_here[j]
        place_j = offset + j
        value = field[place_j]
        image = stencil(
            value,
            above_all[j : j + 1, :],
            below_all[j : j + 1, :],
            0.0,
            0.0,
            field[jnp.minimum(place_j + 1, length - 1)],
            field[jnp.maximum(place_j - 1, 0)],
            weights,
            weight_sum + data_weight + (tau_up + tau_down),
            tau_up,
            tau_down,
        )
        remainder[j] = rhs[j] - image
        copy = pltpu.make_async_copy(remainder.at[j], residual.at[j], sent.at[1, j])
        copy.start()
        copies.append(copy)
    for copy in copies:
        copy.wait()


def body(blocks, slabs, obs_mask, precision, observed, edge_class, temporal_weight, inverse):
    dates_here, lines, all_columns = observed.shape
    dates = inverse.shape[0]
    width = all_columns // blocks
    length = min(dates_here + (1 if blocks == 2 else 2), dates)

    pairs = [(i, i ^ 1) for i in range(slabs)]
    across_pairs = [(i, (i + 1) % slabs) for i in range(1, slabs, 2)]
    across_pairs = across_pairs + [(b, a) for a, b in across_pairs]

    def rotate(value, k):
        return lax.ppermute(value, "dates", [(i, (i + k) % blocks) for i in range(blocks)])

    def swap_rows(first, second):
        return lax.ppermute(first, "rows", pairs), lax.ppermute(second, "rows", across_pairs)

    def swap_ends(ends):
        if blocks == 2:
            other = rotate(ends, 1)
            return other[8:16], other[0:8]
        forward = [(i, i + 1) for i in range(blocks - 1)]
        backward = [(b, a) for a, b in forward]
        return lax.ppermute(ends[8:16], "dates", forward), lax.ppermute(ends[0:8], "dates", backward)

    def send(stack):
        return jnp.stack([rotate(stack[k - 1], k) for k in range(1, blocks)])

    pixel = (dates, lines, width)
    block = (dates_here, lines, all_columns)
    part = (blocks - 1, dates_here, lines, width)
    rows = (dates, width)
    ends_shape = (16, LANES)
    vector = (8, LANES)
    window_shape = (blocks - 1, length, lines, width)
    edges_shape = (blocks - 1, 2 * dates_here, width)

    half = max(dates_here // 2, 1)

    def send_parts(spans):
        return call(
            functools.partial(send_kernel, blocks, spans),
            [(blocks - 1, stop - start, lines, width) for _, start, stop in spans],
            [(part, jnp.int32), part, part, pltpu.SemaphoreType.DMA((blocks - 1, dates_here, 3))],
            [],
            [obs_mask, precision, observed],
            HBM,
        )

    (rhs_part,) = send_parts([("rhs", 0, half)])
    rhs_late_part, weight_part = send_parts([("rhs", half, dates_here), ("weight", 0, dates_here)])
    rhs_other = send(rhs_part)
    rhs_late = send(rhs_late_part)
    weight_other = send(weight_part)


    staged, weight_here, rhs_here, weights, last_row = call(
        stage_kernel,
        [(inverse.shape, inverse.dtype), block, block, (3, lines, all_columns), (lines, all_columns)],
        [
            (block, jnp.int32), block, block, (edge_class.shape, jnp.int32),
            pltpu.SemaphoreType.DMA((dates_here, 3)), pltpu.SemaphoreType.DMA((dates + 1,)),
        ],
        [],
        [obs_mask, precision, observed, edge_class, inverse],
        HBM,
    )
    zero_one = jnp.zeros((1,), jnp.float32)
    tau = jnp.concatenate([zero_one, temporal_weight, zero_one])
    tau = jnp.broadcast_to(tau[:, None], (dates + 1, LANES))

    row_above = lax.ppermute(last_row, "rows", [(i, (i + 1) % slabs) for i in range(slabs)])
    early_shape = (blocks - 1, (length + 1) // 2, lines, width)
    late_shape = (blocks - 1, length // 2, lines, width)
    precond, p_first, p_second, p_ends, p_early, p_late, dot_1 = call(
        functools.partial(first_kernel, blocks),
        [pixel, rows, rows, ends_shape, early_shape, late_shape, vector],
        [pixel],
        [],
        [rhs_here, rhs_other, rhs_late, staged],
    )
    p_second, row_above = lax.optimization_barrier((p_second, row_above))
    p_halo_1, p_halo_2 = swap_rows(p_first, p_second)
    p_left, p_right = swap_ends(p_ends)
    p_early, p_late, p_left, p_halo_2 = lax.optimization_barrier((p_early, p_late, p_left, p_halo_2))
    precond_early = send(p_early)
    precond_late = send(p_late)
    mapped, m_first, m_second, m_ends, m_windows, p_forward, data_weight, dot_2, dot_3 = call(
        functools.partial(second_kernel, blocks),
        [pixel, rows, rows, ends_shape, window_shape, edges_shape, pixel, vector, vector],
        [pixel, vector],
        [],
        [tau, weights, row_above, precond, p_halo_1, p_halo_2, p_left, p_right, weight_here, weight_other, staged],
    )
    m_halo_1, m_halo_2 = swap_rows(m_first, m_second)
    m_ends_other = () if blocks == 2 else swap_ends(m_ends)
    sums, m_forward = call(
        functools.partial(third_kernel, blocks),
        [vector, edges_shape],
        [vector],
        [],
        [tau, weights, row_above, mapped, m_halo_1, m_halo_2, data_weight, dot_1, dot_2, dot_3, *m_ends_other],
    )
    precond_halos = send(p_forward)
    sums, precond_early, precond_late = lax.optimization_barrier((sums, precond_early, precond_late))
    if blocks == 2:
        ends_other, sums_other = rotate(m_ends, 1), rotate(sums, 1)
        (sums,) = call(join_kernel, [vector], [], [], [weights, m_ends, sums, ends_other, sums_other])
    else:
        steps = 1
        while steps < blocks:
            sums = sums + lax.ppermute(sums, "dates", [(i, i ^ steps) for i in range(blocks)])
            steps *= 2
    m_windows, m_forward, precond_halos, sums = lax.optimization_barrier((m_windows, m_forward, precond_halos, sums))
    mapped_halos = send(m_forward)
    mapped_other = send(m_windows)
    steps = 1
    while steps < slabs:
        sums = sums + lax.ppermute(sums, "rows", [(i, i ^ steps) for i in range(slabs)])
        steps *= 2
    return tuple(
        call(
            functools.partial(last_kernel, blocks),
            [block, block],
            [
                (length, lines, all_columns), (dates_here, all_columns), (dates_here, all_columns), block,
                pltpu.SemaphoreType.DMA((2, dates_here)),
            ],
            [],
            [
                tau, weights, row_above, sums, precond, mapped, precond_early, precond_late, mapped_other, p_halo_1, p_halo_2, m_halo_1, m_halo_2,
                precond_halos, mapped_halos, weight_here, rhs_here,
            ],
            out_space=HBM,
        )
    )


def solution(mesh):
    return jax.shard_map(
        functools.partial(body, mesh.shape["dates"], mesh.shape["rows"]),
        mesh=mesh,
        in_specs=(
            P("dates", "rows", None),
            P("dates", "rows", None),
            P("dates", "rows", None),
            P(None, "rows", None),
            P(),
            P(None, None, "rows", "dates"),
        ),
        out_specs=(P("dates", "rows", None), P("dates", "rows", None)),
        check_vma=False,
    )
```

```python
import functools

import jax
import jax.numpy as jnp
from jax import lax
from jax.experimental import pallas as pl
from jax.experimental.pallas import tpu as pltpu
from jax.sharding import PartitionSpec as P

MASS = 0.1
LANES = 128
VMEM = pl.BlockSpec(memory_space=pltpu.VMEM)
SMEM = pl.BlockSpec(memory_space=pltpu.SMEM)
HBM = pl.BlockSpec(memory_space=pltpu.HBM)
PARAMS = pltpu.CompilerParams(vmem_limit_bytes=8 * 1024 * 1024)

COST = pl.CostEstimate(flops=1, bytes_accessed=1, transcendentals=0)


def call(kernel, out_shapes, scratch, scalars, arrays, space=VMEM, out_space=VMEM):
    def typed(entry):
        return entry if isinstance(entry[-1], (jnp.dtype, type)) else (entry, jnp.float32)

    if space is HBM:
        arrays = [pltpu.with_memory_space_constraint(array, pltpu.HBM) for array in arrays]
    return pl.pallas_call(
        kernel,
        out_shape=[jax.ShapeDtypeStruct(*typed(entry)) for entry in out_shapes],
        in_specs=[SMEM] * len(scalars) + [space] * len(arrays),
        out_specs=[out_space] * len(out_shapes),
        scratch_shapes=[pltpu.VMEM(*typed(entry)) if isinstance(entry, tuple) else entry for entry in scratch],
        compiler_params=PARAMS,
        cost_estimate=COST,
    )(*scalars, *arrays)


def tile(index, width=LANES):
    return pl.ds(pl.multiple_of(index * width, LANES), width)


def columns(block, width):
    return pl.ds(pl.multiple_of(block * width, LANES), width)


def row_ids(width):
    return lax.broadcasted_iota(jnp.int32, (8, width), 0)


def lane_ids(width):
    return lax.broadcasted_iota(jnp.int32, (8, width), 1)


def window_start(block, dates_here, length, dates):
    return jnp.clip(block * dates_here - 1, 0, dates - length)


def edge_rows(value, parity):
    top, bottom = value[0:1], value[7:8]
    return jnp.where(parity == 0, bottom, top), jnp.where(parity == 0, top, bottom)


def halo_rows(first, second, parity):
    above = jnp.where(parity == 0, second, first)
    below = jnp.where(parity == 0, first, second)
    return above, below


def stencil(value, above, below, left, right, later, earlier, weights, diagonal, tau_up, tau_down):
    across, across_prev, downward, downward_prev = weights
    width = value.shape[1]
    rows, lanes = row_ids(width), lane_ids(width)
    next_column = jnp.where(lanes == width - 1, right, pltpu.roll(value, width - 1, 1))
    prev_column = jnp.where(lanes == 0, left, pltpu.roll(value, 1, 1))
    next_row = jnp.where(rows == 7, below, pltpu.roll(value, 7, 0))
    prev_row = jnp.where(rows == 0, above, pltpu.roll(value, 1, 0))
    away = across * next_column + across_prev * prev_column
    away = away + downward * next_row + downward_prev * prev_row
    return diagonal * value - (away + tau_up * later + tau_down * earlier)


def apply_inverse(inverse, source, store):
    dates = inverse.shape[0]
    width = source.shape[2]
    step_width = 2 * LANES if width % (2 * LANES) == 0 else LANES

    def step(index, total):
        lanes = tile(index, step_width)
        values = [source[s, :, lanes] for s in range(dates)]
        for t in range(dates):
            mapped = inverse[t, 0, :, lanes].astype(jnp.float32) * values[0]
            for s in range(1, dates):
                mapped = mapped + inverse[t, s, :, lanes].astype(jnp.float32) * values[s]
            total = total + values[t] * mapped
            store(t, lanes, mapped)
        return total

    return fold(lax.fori_loop(0, width // step_width, step, jnp.zeros((8, step_width), jnp.float32)))


def pack_edges(field, parity, first, second, ends):
    dates, _, width = field.shape
    lanes = lane_ids(LANES)
    begin = jnp.zeros((8, LANES), jnp.float32)
    end = begin
    for t in range(dates):
        value = field[t]
        send_1, send_2 = edge_rows(value, parity)
        first[t : t + 1, :] = send_1
        second[t : t + 1, :] = send_2
        begin = jnp.where(lanes == t, value[:, 0:1], begin)
        end = jnp.where(lanes == t, value[:, width - 1 : width], end)
    ends[0:8, :] = begin
    ends[8:16, :] = end


def gather_dates(target, own, received, date_block, blocks, dates_here):
    for j in range(dates_here):
        target[date_block * dates_here + j] = own(j)
    for k in range(1, blocks):
        source = lax.rem(date_block + blocks - k, blocks)
        base = source * dates_here
        for part in received:
            for j in range(part.shape[1]):
                target[base + j] = part[k - 1, j]
            base = base + part.shape[1]


def send_windows(field, parts, date_block, blocks, dates_here):
    length = sum(part.shape[1] for part in parts)
    for k in range(1, blocks):
        target = lax.rem(date_block + k, blocks)
        start = window_start(target, dates_here, length, field.shape[0])
        base = start
        for part in parts:
            for j in range(part.shape[1]):
                part[k - 1, j] = field[base + j]
            base = base + part.shape[1]


def send_kernel(blocks, spans, mask, precision, observed, *refs):
    outputs = refs[: len(spans)]
    masks, precisions, observations, arrived = refs[len(spans) :]
    width = masks.shape[3]
    first = min(start for _, start, _ in spans)
    last = max(stop for _, _, stop in spans)
    for k in range(1, blocks):
        there = columns(lax.rem(lax.axis_index("dates") + k, blocks), width)

        def copies(j):
            sources = [(mask, masks), (precision, precisions)]
            if any(kind == "rhs" and start <= j < stop for kind, start, stop in spans):
                sources.append((observed, observations))
            return [
                pltpu.make_async_copy(source.at[j, :, there], target.at[k - 1, j], arrived.at[k - 1, j, index])
                for index, (source, target) in enumerate(sources)
            ]

        for j in range(first, last):
            for copy in copies(j):
                copy.start()
        for j in range(first, last):
            for copy in copies(j):
                copy.wait()
            value = masks[k - 1, j].astype(jnp.float32) * precisions[k - 1, j]
            for (kind, start, stop), output in zip(spans, outputs):
                if start <= j < stop:
                    output[k - 1, j - start] = value * observations[k - 1, j] if kind == "rhs" else value


def stage_kernel(
    mask, precision, observed, edge_class, inverse, staged, weight, rhs, weights, last_row, masks, precisions, observations, classes, arrived, loaded
):
    dates_here = mask.shape[0]
    dates = inverse.shape[0]
    loads = [pltpu.make_async_copy(edge_class, classes, loaded.at[dates])]
    loads += [pltpu.make_async_copy(inverse.at[t], staged.at[t], loaded.at[t]) for t in range(dates)]
    copies = [
        [
            pltpu.make_async_copy(source.at[j], target.at[j], arrived.at[j, index])
            for index, (source, target) in enumerate(((mask, masks), (precision, precisions), (observed, observations)))
        ]
        for j in range(dates_here)
    ]
    for group in copies:
        for copy in group:
            copy.start()
    for load in loads:
        load.start()
    for j, group in enumerate(copies):
        for copy in group:
            copy.wait()
        value = masks[j].astype(jnp.float32) * precisions[j]
        weight[j] = value
        rhs[j] = value * observations[j]
    loads[0].wait()
    width = weights.shape[2]
    lanes = lane_ids(width)
    across = jnp.where(lanes == width - 1, 0.0, 0.25 * (classes[0].astype(jnp.float32) + 1.0))
    weights[0] = across
    weights[1] = jnp.where(lanes == 0, 0.0, pltpu.roll(across, 1, 1))
    downward = 0.25 * (classes[1].astype(jnp.float32) + 1.0)
    weights[2] = downward
    last_row[...] = jnp.broadcast_to(downward[7:8], downward.shape)
    for load in loads[1:]:
        load.wait()


def forward_halos(halo_1, halo_2, forwarded, date_block, blocks):
    dates_here = forwarded.shape[1] // 2
    for k in range(1, blocks):
        target = lax.rem(date_block + k, blocks)
        for j in range(dates_here):
            date = pl.ds(target * dates_here + j, 1)
            forwarded[k - 1, j : j + 1, :] = halo_1[date, :]
            forwarded[k - 1, dates_here + j : dates_here + j + 1, :] = halo_2[date, :]


def first_kernel(blocks, rhs_here, early, late, inverse, precond, first, second, ends, early_windows, late_windows, dot, rhs):
    date_block, parity = lax.axis_index("dates"), lax.rem(lax.axis_index("rows"), 2)
    dates_here = rhs_here.shape[0]
    here = columns(date_block, rhs.shape[2])
    gather_dates(rhs, lambda j: rhs_here[j, :, here], (early, late), date_block, blocks, dates_here)

    def store(t, lanes, value):
        precond[t, :, lanes] = value

    dot[...] = apply_inverse(inverse, rhs, store)
    pack_edges(precond, parity, first, second, ends)
    send_windows(precond, (early_windows, late_windows), date_block, blocks, dates_here)


def edge_weights(weights_all, above, lanes):
    across, across_prev, downward = [weights_all[k, :, lanes] for k in range(3)]
    width = across.shape[1]
    rows = row_ids(width)
    downward = jnp.where((rows == 7) & (lax.axis_index("rows") == lax.axis_size("rows") - 1), 0.0, downward)
    row_above = jnp.where(lax.axis_index("rows") == 0, 0.0, above[0:1, lanes])
    downward_prev = jnp.where(rows == 0, row_above, pltpu.roll(downward, 1, 0))
    weights = (across, across_prev, downward, downward_prev)
    return weights, MASS + across + across_prev + downward + downward_prev


def pixel_image(tau, weights_all, row_above, field, halo_1, halo_2, ends_left, ends_right, data_weight, use):
    date_block, parity = lax.axis_index("dates"), lax.rem(lax.axis_index("rows"), 2)
    dates, _, width = field.shape
    here = columns(date_block, width)
    weights, weight_sum = edge_weights(weights_all, row_above, here)
    for t in range(dates):
        above, below = halo_rows(halo_1[t : t + 1, :], halo_2[t : t + 1, :], parity)
        tau_up, tau_down = spread(tau, t + 1, width), spread(tau, t, width)
        value = field[t]
        diagonal = weight_sum + data_weight[t] + (tau_up + tau_down)
        image = stencil(
            value,
            above,
            below,
            0.0 if ends_left is None else ends_left[:, t : t + 1],
            0.0 if ends_right is None else ends_right[:, t : t + 1],
            field[min(t + 1, dates - 1)],
            field[max(t - 1, 0)],
            weights,
            diagonal,
            tau_up,
            tau_down,
        )
        use(t, value, image)


def spread(tau, index, width):
    return jnp.tile(jnp.broadcast_to(tau[pl.ds(index, 1), :], (8, LANES)), (1, width // LANES))


def fold(value):
    total = value[:, :LANES]
    for index in range(1, value.shape[1] // LANES):
        total = total + value[:, index * LANES : (index + 1) * LANES]
    return total


def second_kernel(
    blocks, tau, weights, row_above, precond, halo_1, halo_2, ends_left, ends_right, weight_here, received, inverse,
    mapped, first, second, ends, windows, forwarded, data_weight, dot_image, dot_mapped, image_all, total,
):
    date_block, parity = lax.axis_index("dates"), lax.rem(lax.axis_index("rows"), 2)
    dates_here = weight_here.shape[0]
    here = columns(date_block, precond.shape[2])
    gather_dates(data_weight, lambda j: weight_here[j, :, here], (received,), date_block, blocks, dates_here)
    total[...] = jnp.zeros_like(total)

    def use(t, value, image):
        image_all[t] = image
        total[...] = total[...] + fold(value * image)

    pixel_image(tau, weights, row_above, precond, halo_1, halo_2, ends_left, ends_right, data_weight, use)
    dot_image[...] = total[...]

    def store(t, lanes, value):
        mapped[t, :, lanes] = value

    dot_mapped[...] = apply_inverse(inverse, image_all, store)
    pack_edges(mapped, parity, first, second, ends)
    send_windows(mapped, (windows,), date_block, blocks, dates_here)
    forward_halos(halo_1, halo_2, forwarded, date_block, blocks)


def third_kernel(
    blocks, tau, weights, row_above, mapped, halo_1, halo_2, data_weight, dot_1, dot_2, dot_3, *refs,
):
    *ends, sums, forwarded, total = refs
    left, right = ends if blocks != 2 else (None, None)
    total[...] = jnp.zeros_like(total)

    def use(t, value, image):
        total[...] = total[...] + fold(value * image)

    pixel_image(tau, weights, row_above, mapped, halo_1, halo_2, left, right, data_weight, use)
    rows = row_ids(LANES)
    result = jnp.zeros((8, LANES), jnp.float32)
    for index, dot in enumerate((dot_1, dot_2, dot_3, total)):
        result = jnp.where(rows == index, jnp.sum(dot[...]), result)
    if blocks == 2:
        sums[0:16, :] = ends[0][...]
        sums[16:24, :] = result
    else:
        sums[...] = result
    forward_halos(halo_1, halo_2, forwarded, lax.axis_index("dates"), blocks)


def join_kernel(weights, here, other, joined):
    width = weights.shape[2] // 2
    boundary = weights[0, :, width - LANES : width][:, LANES - 1 : LANES]
    dates = jnp.where(lax.axis_index("dates") == 0, here[8:16, :] * other[0:8, :], here[0:8, :] * other[8:16, :])
    crossing = -2.0 * jnp.sum(boundary * dates)
    joined[...] = here[16:24, :] + other[16:24, :] + jnp.where(row_ids(LANES) == 3, crossing, 0.0)


def last_kernel(
    blocks, tau, weights_all, row_above, sums, precond, mapped, precond_early, precond_late, mapped_other, own_p1, own_p2, own_m1, own_m2,
    precond_halos, mapped_halos, weight_here, rhs, solution, residual, field, above_all, below_all, remainder, sent,
):
    date_block, parity = lax.axis_index("dates"), lax.rem(lax.axis_index("rows"), 2)
    dates, _, width = precond.shape
    dates_here, _, all_columns = rhs.shape
    length = field.shape[0]
    one = sums[0:1, :]
    two = sums[1:2, :]
    three = sums[2:3, :]
    four = sums[3:4, :]
    alpha = one / two
    rz = alpha * alpha * three - one
    ahead = 1.0 + rz / one
    curve = ahead * ahead * two - 2.0 * ahead * alpha * three + alpha * alpha * four
    alpha_last = rz / curve
    scale_p = jnp.tile(alpha + alpha_last * ahead, (1, width // LANES))
    scale_m = jnp.tile(-alpha_last * alpha, (1, width // LANES))

    def mix(p, m):
        return scale_p * p + scale_m * m

    start = window_start(date_block, dates_here, length, dates)
    offset = date_block * dates_here - start
    here = columns(date_block, width)
    for j in range(length):
        field[j, :, here] = mix(precond[start + j], mapped[start + j])
    first_date = date_block * dates_here

    def own(rows):
        if dates_here % 8 == 0:
            return rows[pl.ds(pl.multiple_of(first_date, 8), dates_here), :]
        return jnp.concatenate([rows[pl.ds(first_date + j, 1), :] for j in range(dates_here)], axis=0)

    above, below = halo_rows(mix(own(own_p1), own(own_m1)), mix(own(own_p2), own(own_m2)), parity)
    above_all[:, here] = above
    below_all[:, here] = below
    for k in range(1, blocks):
        there = columns(lax.rem(date_block + blocks - k, blocks), width)
        for j in range(length):
            count = precond_early.shape[1]
            other = precond_early[k - 1, j] if j < count else precond_late[k - 1, j - count]
            field[j, :, there] = mix(other, mapped_other[k - 1, j])
        above, below = halo_rows(
            mix(precond_halos[k - 1, :dates_here, :], mapped_halos[k - 1, :dates_here, :]),
            mix(precond_halos[k - 1, dates_here:, :], mapped_halos[k - 1, dates_here:, :]),
            parity,
        )
        above_all[:, there] = above
        below_all[:, there] = below
    copies = [pltpu.make_async_copy(field.at[offset + j], solution.at[j], sent.at[0, j]) for j in range(dates_here)]
    for copy in copies:
        copy.start()
    weights, weight_sum = edge_weights(weights_all, row_above, slice(None))
    for j in range(dates_here):
        date = date_block * dates_here + j
        tau_up, tau_down = spread(tau, date + 1, all_columns), spread(tau, date, all_columns)
        data_weight = weight_here[j]
        place_j = offset + j
        value = field[place_j]
        image = stencil(
            value,
            above_all[j : j + 1, :],
            below_all[j : j + 1, :],
            0.0,
            0.0,
            field[jnp.minimum(place_j + 1, length - 1)],
            field[jnp.maximum(place_j - 1, 0)],
            weights,
            weight_sum + data_weight + (tau_up + tau_down),
            tau_up,
            tau_down,
        )
        remainder[j] = rhs[j] - image
        copy = pltpu.make_async_copy(remainder.at[j], residual.at[j], sent.at[1, j])
        copy.start()
        copies.append(copy)
    for copy in copies:
        copy.wait()


def body(blocks, slabs, obs_mask, precision, observed, edge_class, temporal_weight, inverse):
    dates_here, lines, all_columns = observed.shape
    dates = inverse.shape[0]
    width = all_columns // blocks
    length = min(dates_here + (1 if blocks == 2 else 2), dates)

    pairs = [(i, i ^ 1) for i in range(slabs)]
    across_pairs = [(i, (i + 1) % slabs) for i in range(1, slabs, 2)]
    across_pairs = across_pairs + [(b, a) for a, b in across_pairs]

    def rotate(value, k):
        return lax.ppermute(value, "dates", [(i, (i + k) % blocks) for i in range(blocks)])

    def swap_rows(first, second):
        return lax.ppermute(first, "rows", pairs), lax.ppermute(second, "rows", across_pairs)

    def swap_ends(ends):
        if blocks == 2:
            other = rotate(ends, 1)
            return other[8:16], other[0:8]
        forward = [(i, i + 1) for i in range(blocks - 1)]
        backward = [(b, a) for a, b in forward]
        return lax.ppermute(ends[8:16], "dates", forward), lax.ppermute(ends[0:8], "dates", backward)

    def send(stack):
        return jnp.stack([rotate(stack[k - 1], k) for k in range(1, blocks)])

    pixel = (dates, lines, width)
    block = (dates_here, lines, all_columns)
    part = (blocks - 1, dates_here, lines, width)
    rows = (dates, width)
    ends_shape = (16, LANES)
    vector = (8, LANES)
    window_shape = (blocks - 1, length, lines, width)
    edges_shape = (blocks - 1, 2 * dates_here, width)

    half = max(dates_here // 2, 1)

    def send_parts(spans):
        return call(
            functools.partial(send_kernel, blocks, spans),
            [(blocks - 1, stop - start, lines, width) for _, start, stop in spans],
            [(part, jnp.int32), part, part, pltpu.SemaphoreType.DMA((blocks - 1, dates_here, 3))],
            [],
            [obs_mask, precision, observed],
            HBM,
        )

    (rhs_part,) = send_parts([("rhs", 0, half)])
    rhs_late_part, weight_part = send_parts([("rhs", half, dates_here), ("weight", 0, dates_here)])
    rhs_other = send(rhs_part)
    rhs_late = send(rhs_late_part)
    weight_other = send(weight_part)


    staged, weight_here, rhs_here, weights, last_row = call(
        stage_kernel,
        [(inverse.shape, inverse.dtype), block, block, (3, lines, all_columns), (lines, all_columns)],
        [
            (block, jnp.int32), block, block, (edge_class.shape, jnp.int32),
            pltpu.SemaphoreType.DMA((dates_here, 3)), pltpu.SemaphoreType.DMA((dates + 1,)),
        ],
        [],
        [obs_mask, precision, observed, edge_class, inverse],
        HBM,
    )
    zero_one = jnp.zeros((1,), jnp.float32)
    tau = jnp.concatenate([zero_one, temporal_weight, zero_one])
    tau = jnp.broadcast_to(tau[:, None], (dates + 1, LANES))

    row_above = lax.ppermute(last_row, "rows", [(i, (i + 1) % slabs) for i in range(slabs)])
    early_shape = (blocks - 1, (length + 1) // 2, lines, width)
    late_shape = (blocks - 1, length // 2, lines, width)
    precond, p_first, p_second, p_ends, p_early, p_late, dot_1 = call(
        functools.partial(first_kernel, blocks),
        [pixel, rows, rows, ends_shape, early_shape, late_shape, vector],
        [pixel],
        [],
        [rhs_here, rhs_other, rhs_late, staged],
    )
    p_second, row_above = lax.optimization_barrier((p_second, row_above))
    p_halo_1, p_halo_2 = swap_rows(p_first, p_second)
    p_left, p_right = swap_ends(p_ends)
    p_early, p_late, p_left, p_halo_2 = lax.optimization_barrier((p_early, p_late, p_left, p_halo_2))
    precond_early = send(p_early)
    precond_late = send(p_late)
    mapped, m_first, m_second, m_ends, m_windows, p_forward, data_weight, dot_2, dot_3 = call(
        functools.partial(second_kernel, blocks),
        [pixel, rows, rows, ends_shape, window_shape, edges_shape, pixel, vector, vector],
        [pixel, vector],
        [],
        [tau, weights, row_above, precond, p_halo_1, p_halo_2, p_left, p_right, weight_here, weight_other, staged],
    )
    m_halo_1, m_halo_2 = swap_rows(m_first, m_second)
    m_ends_other = (m_ends,) if blocks == 2 else swap_ends(m_ends)
    sums, m_forward = call(
        functools.partial(third_kernel, blocks),
        [(24, LANES) if blocks == 2 else vector, edges_shape],
        [vector],
        [],
        [tau, weights, row_above, mapped, m_halo_1, m_halo_2, data_weight, dot_1, dot_2, dot_3, *m_ends_other],
    )
    precond_halos = send(p_forward)
    sums, precond_early, precond_late = lax.optimization_barrier((sums, precond_early, precond_late))
    if blocks == 2:
        (sums,) = call(join_kernel, [vector], [], [], [weights, sums, rotate(sums, 1)])
    else:
        steps = 1
        while steps < blocks:
            sums = sums + lax.ppermute(sums, "dates", [(i, i ^ steps) for i in range(blocks)])
            steps *= 2
    m_windows, m_forward, precond_halos, sums = lax.optimization_barrier((m_windows, m_forward, precond_halos, sums))
    mapped_halos = send(m_forward)
    mapped_other = send(m_windows)
    steps = 1
    while steps < slabs:
        sums = sums + lax.ppermute(sums, "rows", [(i, i ^ steps) for i in range(slabs)])
        steps *= 2
    return tuple(
        call(
            functools.partial(last_kernel, blocks),
            [block, block],
            [
                (length, lines, all_columns), (dates_here, all_columns), (dates_here, all_columns), block,
                pltpu.SemaphoreType.DMA((2, dates_here)),
            ],
            [],
            [
                tau, weights, row_above, sums, precond, mapped, precond_early, precond_late, mapped_other, p_halo_1, p_halo_2, m_halo_1, m_halo_2,
                precond_halos, mapped_halos, weight_here, rhs_here,
            ],
            out_space=HBM,
        )
    )


def solution(mesh):
    return jax.shard_map(
        functools.partial(body, mesh.shape["dates"], mesh.shape["rows"]),
        mesh=mesh,
        in_specs=(
            P("dates", "rows", None),
            P("dates", "rows", None),
            P("dates", "rows", None),
            P(None, "rows", None),
            P(),
            P(None, None, "rows", "dates"),
        ),
        out_specs=(P("dates", "rows", None), P("dates", "rows", None)),
        check_vma=False,
    )
```
